512 devices in a mesh: section: 8 (over y), tp: 8 (over z), ctx: 8 (over x, core).
Axes of the slice: x: 4, y: 8, z: 8, core: 2. Of those that a mesh axis runs over, the one named last changes fastest.
Arguments:
- hidden: bfloat16 [32, 4096], P('section', 'ctx'), may hold values from -60 to 60
- gain: float32 [8, 4096], P('section', 'ctx'), may hold values from 0.1 to 1.9
- w_query: bfloat16 [8, 4096, 4096], P('section', 'ctx', 'tp'), may hold values from -0.09375 to 0.09375
- key_weight: bfloat16 [8, 4096, 1024], P('section', 'ctx', 'tp'), may hold values from -0.09375 to 0.09375
- value_weight: bfloat16 [8, 4096, 1024], P('section', 'ctx', 'tp'), may hold values from -0.09375 to 0.09375
- w_out: bfloat16 [8, 4096, 4096], P('section', ('tp', 'ctx')), may hold values from -1.5 to 1.5
- key_cache_slots: bfloat16 [32, 8192, 1024], P('section', 'ctx', 'tp'), may hold values from -64 to 64
- value_cache_slots: bfloat16 [32, 8192, 1024], P('section', 'ctx', 'tp'), may hold values from -6 to 6
- lengths: int32 [32], P('section'), may hold values from 1024 to 8192, as said below
- plan: int32 [32, 8, 2], P('section', 'ctx'), may hold values from 0 to 8192, as said below
- routing: int32 [8, 4], P('section'), may hold values from 0 to 3, each once within a row
Outputs:
- handed: bfloat16 [32, 4096], P('section', 'ctx')
- attn_out: float32 [32, 4096], P('section', 'ctx')
The draws below stay inside these ranges and needn't reach their ends.
Inputs may be any that keep to these rules, and one draw needn't show every extreme that they name: `lengths`: in every section one request has the longest context, 8192. `plan`: for each request the spans [start, end) of the ctx indices follow one another in index order from 0 to the request's length; each holds at most 1024 positions, and some request of every section holds 1024 on every index. Slot j of span c holds position start + j; slots at or past end - start are not in the context. `routing`: each section's row names every row of the previous section's block once.
All inputs are finite; a program needn't handle non-finite values.
Results may differ from the reference program's by a relative error of at most 0.009.
Values may be sent and summed in bfloat16 or wider, within the bound.
No kernel may reach another device: no remote copies, remote signals or barrier semaphores. Data moves between devices by JAX's collectives and lax.ppermute only.
A program may use at most 64 MiB of HBM per device.

```python
import jax
import jax.numpy as jnp
from jax import lax

MODEL_DIM = 4096
QUERY_HEAD_COUNT = 32
KEY_HEADS = 8
HEAD_SIZE = 128
SECTION_REQUESTS = 4
SLOTS_PER_SHARD = 1024
SECTION_COUNT = 8
TOTAL_REQUESTS = 32
REQUEST_SLOTS = 8192
N_SECTION = 8
N_CTX = 8


def split_plan(key):
    total_slots = N_CTX * SLOTS_PER_SHARD
    length_key, longest_key, offset_key = jax.random.split(key, 3)
    lengths = jax.random.randint(length_key, (N_SECTION, SECTION_REQUESTS), max(1, total_slots // 8), total_slots + 1)
    longest = jax.random.randint(longest_key, (N_SECTION, 1), 0, SECTION_REQUESTS)
    lengths = jnp.where(jnp.arange(SECTION_REQUESTS)[None, :] == longest, total_slots, lengths)
    offsets = jax.random.randint(offset_key, (N_SECTION, SECTION_REQUESTS, 1), 0, N_CTX)
    fill_order = (jnp.arange(N_CTX)[None, None, :] - offsets) % N_CTX
    counts = jnp.clip(lengths[:, :, None] - fill_order * SLOTS_PER_SHARD, 0, SLOTS_PER_SHARD)
    span_ends = jnp.cumsum(counts, axis=-1)
    starts = span_ends - counts
    bounds = jnp.stack([starts, span_ends], axis=-1).reshape(N_SECTION * SECTION_REQUESTS, N_CTX, 2)
    return (lengths.reshape(N_SECTION * SECTION_REQUESTS).astype(jnp.int32), bounds.astype(jnp.int32))


def draw_lengths(key, part):
    return split_plan(key)[0]


def draw_plan(key, part):
    return split_plan(key)[1]


def draw_hidden(key, part):
    key = jax.random.fold_in(key, 5)
    noise_key = jax.random.fold_in(key, 0)
    array_shape = (SECTION_REQUESTS * N_SECTION, MODEL_DIM)
    column = jnp.arange(MODEL_DIM, dtype=jnp.float32) / MODEL_DIM
    entries = jax.random.normal(noise_key, array_shape, jnp.float32) * (3.0 ** column)[None, :]
    return jnp.clip(entries, -60.0, 60.0).astype(jnp.bfloat16)


def draw_key_cache_slots(key, part):
    key = jax.random.fold_in(key, 11)
    base_key = jax.random.fold_in(key, 0)
    array_shape = (SECTION_REQUESTS * N_SECTION, N_CTX * SLOTS_PER_SHARD, KEY_HEADS * HEAD_SIZE)
    result = jnp.clip(jax.random.normal(base_key, array_shape, jnp.float32) * 0.5, -3.0, 3.0)
    return jnp.clip(result, -64.0, 64.0).astype(jnp.bfloat16)


def spiked(drawn, stream_key, source, target, parts, factor):
    owner, partner = [(jnp.arange(drawn.shape[dim]) // (drawn.shape[dim] // parts)).reshape([-1 if axis == dim else 1 for axis in range(drawn.ndim)]) for dim in (source, target)]
    chosen = jax.random.permutation(stream_key, parts)[partner]
    strong = (owner == chosen) | (owner == (partner + parts // 2) % parts)
    return jnp.where(strong, factor * drawn, drawn)


def block_levels(stream_key, dims, pieces, least, largest):
    def one(axis_at, shards_of):
        steps = jax.random.uniform(jax.random.fold_in(jax.random.fold_in(stream_key, 6), axis_at), (shards_of,), jnp.float32, least / len(pieces), largest / len(pieces))
        return jnp.repeat(jnp.exp(steps), dims[axis_at] // shards_of).reshape((-1,) + (1,) * (len(dims) - axis_at - 1))

    level = one(*pieces[0])
    for cut in pieces[1:]:
        level = level * one(*cut)
    return level


def noise(stream_key, shape, spread, bound, cuts=(), held_as=jnp.bfloat16):
    array = jax.random.normal(stream_key, shape, jnp.float32) * spread
    if len(cuts) > 0:
        array = block_levels(stream_key, shape, cuts, -0.22, 0.18) * array
    return jnp.clip(array, min=-bound, max=bound).astype(held_as)


def bell_draw_with(rng, extent, scale, most, cuts, heavy, held_as=jnp.bfloat16):
    values = scale * jax.random.normal(rng, extent, jnp.float32)
    if cuts:
        values = values * block_levels(rng, extent, cuts, -0.22, 0.18)
    return jnp.clip(spiked(values, jax.random.fold_in(rng, 3), *heavy), -most, most).astype(held_as)


def setup_inputs(seed: int = 0) -> dict:
    seeds = jax.random.split(jax.random.key(seed), 12)
    return {
        "hidden": draw_hidden(jax.random.fold_in(seeds[11], 71), 0),
        "gain": jnp.clip(1.0 + 0.18 * jax.random.normal(seeds[1], (SECTION_COUNT, MODEL_DIM), jnp.float32), 0.1, 1.9),
        "w_query": noise(seeds[2], (SECTION_COUNT, MODEL_DIM, QUERY_HEAD_COUNT * HEAD_SIZE), MODEL_DIM ** -0.5, 0.09375, ((0, 8), (1, 8), (2, 8))),
        "key_weight": noise(seeds[3], (SECTION_COUNT, MODEL_DIM, KEY_HEADS * HEAD_SIZE), MODEL_DIM ** -0.5, 0.09375, ((0, 8), (1, 8), (2, 8))),
        "value_weight": noise(seeds[4], (SECTION_COUNT, MODEL_DIM, KEY_HEADS * HEAD_SIZE), MODEL_DIM ** -0.5, 0.09375, ((0, 8), (1, 8), (2, 8))),
        "w_out": bell_draw_with(seeds[5], (SECTION_COUNT, QUERY_HEAD_COUNT * HEAD_SIZE, MODEL_DIM), HEAD_SIZE ** -0.5, 1.5, ((0, 8), (1, 64)), (1, 2, 64, 4.0)),
        "key_cache_slots": draw_key_cache_slots(jax.random.fold_in(seeds[11], 71), 0),
        "value_cache_slots": noise(seeds[7], (TOTAL_REQUESTS, REQUEST_SLOTS, KEY_HEADS * HEAD_SIZE), 1.0, 6.0, ((0, 8), (1, 8), (2, 8))),
        "lengths": draw_lengths(jax.random.fold_in(seeds[11], 71), 0),
        "plan": draw_plan(jax.random.fold_in(seeds[11], 71), 0),
        "routing": jax.vmap(lambda own: jax.random.permutation(own, SECTION_REQUESTS))(jax.random.split(seeds[10], SECTION_COUNT)).reshape((SECTION_COUNT, SECTION_REQUESTS)).astype(jnp.int32),
    }


EPSILON = 1e-05
NEGATIVE = -1e+30
ROPE_BASE = 500000.0

def apply_rotary(values, position):
    half_dim = values.shape[-1] // 2
    frequency = ROPE_BASE ** (-2.0 * jnp.arange(half_dim, dtype=jnp.float32) / values.shape[-1])
    angles = position.astype(jnp.float32)[:, None, None] * frequency
    cosine = jnp.cos(angles)
    sine_value = jnp.sin(angles)
    lower_half = values[..., :half_dim]
    upper_half = values[..., half_dim:]
    return jnp.concatenate([lower_half * cosine - upper_half * sine_value, upper_half * cosine + lower_half * sine_value], axis=-1)

def section_layer(hidden, gain, w_query, key_weight, value_weight, w_out, key_cache_slots, value_cache_slots, lengths, plan):
    request_count = hidden.shape[0]
    hidden_f = hidden.astype(jnp.float32)
    mean_square = lax.optimization_barrier(jnp.mean(hidden_f * hidden_f, axis=1))
    inverse = lax.rsqrt(mean_square + EPSILON)[:, None]
    scaled_in = (hidden_f * gain.astype(jnp.float32)).astype(jnp.bfloat16)
    query_raw = jnp.dot(scaled_in, w_query, preferred_element_type=jnp.float32) * inverse
    unrotated_key = jnp.dot(scaled_in, key_weight, preferred_element_type=jnp.float32) * inverse
    projected_value = jnp.dot(scaled_in, value_weight, preferred_element_type=jnp.float32) * inverse
    rotated_query = apply_rotary(query_raw.reshape(request_count, QUERY_HEAD_COUNT, HEAD_SIZE), lengths).astype(jnp.bfloat16)
    fresh_key = apply_rotary(unrotated_key.reshape(request_count, KEY_HEADS, HEAD_SIZE), lengths).astype(jnp.bfloat16)
    fresh_value = projected_value.reshape(request_count, KEY_HEADS, HEAD_SIZE).astype(jnp.bfloat16)
    group_count = QUERY_HEAD_COUNT // KEY_HEADS
    query_by_group = rotated_query.reshape(request_count, KEY_HEADS, group_count, HEAD_SIZE).astype(jnp.float32)
    stored_keys = key_cache_slots.reshape(request_count, N_CTX, SLOTS_PER_SHARD, KEY_HEADS, HEAD_SIZE).astype(jnp.float32)
    stored_values = value_cache_slots.reshape(request_count, N_CTX, SLOTS_PER_SHARD, KEY_HEADS, HEAD_SIZE).astype(jnp.float32)
    scores = jnp.einsum('rkgd,rcjkd->rkgcj', query_by_group, stored_keys) * HEAD_SIZE ** (-0.5)
    counts = plan[:, :, 1] - plan[:, :, 0]
    live_slot = (jnp.arange(SLOTS_PER_SHARD, dtype=jnp.int32)[None, None, :] < counts[:, :, None])[:, None, None, :, :]
    masked = jnp.where(live_slot, scores, NEGATIVE)
    block_max = lax.optimization_barrier(jnp.max(masked, axis=-1))
    weights = jnp.where(live_slot, jnp.exp(masked - block_max[..., None]), 0.0)
    block_sum = lax.optimization_barrier(jnp.sum(weights, axis=-1))
    weights_bf = lax.optimization_barrier(weights.astype(jnp.bfloat16))
    block_out = jnp.einsum('rkgcj,rcjkd->rkgcd', weights_bf.astype(jnp.float32), stored_values)
    new_score = jnp.einsum('rkgd,rkd->rkg', query_by_group, fresh_key.astype(jnp.float32)) * HEAD_SIZE ** (-0.5)
    peak = jnp.maximum(lax.optimization_barrier(jnp.max(block_max, axis=-1)), new_score)
    old_factor = jnp.exp(block_max - peak[..., None])
    new_factor = jnp.exp(new_score - peak)
    total_sum = lax.optimization_barrier(jnp.sum(block_sum * old_factor, axis=-1)) + new_factor
    merged = lax.optimization_barrier(jnp.sum(block_out * old_factor[..., None], axis=-2)) + new_factor[..., None] * fresh_value.astype(jnp.float32)[:, :, None, :]
    attended = (merged / total_sum[..., None]).astype(jnp.bfloat16).reshape(request_count, QUERY_HEAD_COUNT * HEAD_SIZE)
    branch_out = jnp.dot(attended, w_out, preferred_element_type=jnp.float32)
    section_rows = (hidden_f + branch_out).astype(jnp.bfloat16)
    return (section_rows, branch_out)

def reference(hidden, gain, w_query, key_weight, value_weight, w_out, key_cache_slots, value_cache_slots, lengths, plan, routing):
    section_list = []
    branch_list = []
    for section_number in range(N_SECTION):
        first_row = section_number * SECTION_REQUESTS
        last_row = first_row + SECTION_REQUESTS
        rows_out, branch_out = section_layer(hidden[first_row:last_row], gain[section_number], w_query[section_number], key_weight[section_number], value_weight[section_number], w_out[section_number], key_cache_slots[first_row:last_row], value_cache_slots[first_row:last_row], lengths[first_row:last_row], plan[first_row:last_row])
        section_list.append(rows_out)
        branch_list.append(branch_out)
    handed_list = []
    for section_number in range(N_SECTION):
        source = section_list[(section_number - 1) % N_SECTION]
        handed_list.append(source[routing[section_number]])
    return (jnp.concatenate(handed_list, axis=0), jnp.concatenate(branch_list, axis=0))
```

```python
import jax
import jax.numpy as jnp
from jax import lax
from jax.sharding import PartitionSpec as P

HEAD_SIZE = 128


EPSILON = 1e-05
NEGATIVE = -1e30
ROPE_BASE = 500000.0


def from_behind(value, axis, steps):
    count = lax.axis_size(axis)
    pairs = [(source, (source + steps) % count) for source in range(count)]
    return lax.ppermute(value, axis, pairs)


def spread(value, axis):
    copies = jnp.broadcast_to(value[None], (lax.axis_size(axis),) + value.shape)
    return lax.all_to_all(copies, axis, 0, 0, tiled=True)


def apply_rotary(values, position):
    half_dim = values.shape[-1] // 2
    frequency = ROPE_BASE ** (-2.0 * jnp.arange(half_dim, dtype=jnp.float32) / values.shape[-1])
    angles = position.astype(jnp.float32)[:, None, None] * frequency
    cosine = jnp.cos(angles)
    sine_value = jnp.sin(angles)
    lower_half = values[..., :half_dim]
    upper_half = values[..., half_dim:]
    return jnp.concatenate(
        [
            lower_half * cosine - upper_half * sine_value,
            upper_half * cosine + lower_half * sine_value,
        ],
        axis=-1,
    )


def per_device(
    hidden,
    gain,
    w_query,
    key_weight,
    value_weight,
    w_out,
    key_cache_slots,
    value_cache_slots,
    lengths,
    plan,
    routing,
):
    request_count = hidden.shape[0]
    model_width = hidden.shape[1] * lax.axis_size("ctx")
    hidden_f = hidden.astype(jnp.float32)
    scaled_in = (hidden_f * gain[0]).astype(jnp.bfloat16)
    squares = jnp.sum(hidden_f * hidden_f, axis=1)
    query_part = jnp.dot(scaled_in, w_query[0], preferred_element_type=jnp.float32)
    key_part = jnp.dot(scaled_in, key_weight[0], preferred_element_type=jnp.float32)
    value_part = jnp.dot(scaled_in, value_weight[0], preferred_element_type=jnp.float32)
    packed = jnp.concatenate([query_part, key_part, value_part, squares[:, None]], axis=1)
    packed = spread(packed, "ctx").sum(axis=0)
    query_width, key_width = query_part.shape[1], key_part.shape[1]
    query_part = packed[:, :query_width]
    key_part = packed[:, query_width : query_width + key_width]
    value_part = packed[:, query_width + key_width : query_width + 2 * key_width]
    squares = packed[:, query_width + 2 * key_width]
    inverse = lax.rsqrt(squares / model_width + EPSILON)[:, None]
    kv_heads = key_part.shape[1] // HEAD_SIZE
    query_heads = query_part.shape[1] // HEAD_SIZE
    group_count = query_heads // kv_heads
    rotated_query = apply_rotary(
        (query_part * inverse).reshape(request_count, query_heads, HEAD_SIZE), lengths
    ).astype(jnp.bfloat16)
    fresh_key = apply_rotary(
        (key_part * inverse).reshape(request_count, kv_heads, HEAD_SIZE), lengths
    ).astype(jnp.bfloat16)
    fresh_value = (
        (value_part * inverse).reshape(request_count, kv_heads, HEAD_SIZE).astype(jnp.bfloat16)
    )
    query_by_group = rotated_query.reshape(request_count, kv_heads, group_count, HEAD_SIZE)
    slot_count = key_cache_slots.shape[1]
    stored_keys = key_cache_slots.reshape(request_count, slot_count, kv_heads, HEAD_SIZE)
    stored_values = value_cache_slots.reshape(request_count, slot_count, kv_heads, HEAD_SIZE)
    scores = jnp.einsum(
        "rkgd,rjkd->rkgj", query_by_group, stored_keys, preferred_element_type=jnp.float32
    ) * HEAD_SIZE ** (-0.5)
    counts = plan[:, 0, 1] - plan[:, 0, 0]
    live_slot = (jnp.arange(slot_count, dtype=jnp.int32)[None, :] < counts[:, None])[
        :, None, None, :
    ]
    masked = jnp.where(live_slot, scores, NEGATIVE)
    block_max = jnp.max(masked, axis=-1)
    weights = jnp.where(live_slot, jnp.exp(masked - block_max[..., None]), 0.0)
    block_sum = jnp.sum(weights, axis=-1)
    block_out = jnp.einsum(
        "rkgj,rjkd->rkgd",
        weights.astype(jnp.bfloat16),
        stored_values,
        preferred_element_type=jnp.float32,
    )
    new_score = jnp.einsum(
        "rkgd,rkd->rkg", query_by_group, fresh_key, preferred_element_type=jnp.float32
    ) * HEAD_SIZE ** (-0.5)
    ctx_count, ctx_index = lax.axis_size("ctx"), lax.axis_index("ctx")
    column_width = query_heads * HEAD_SIZE // ctx_count
    parts_per_head = HEAD_SIZE // column_width

    def by_owner(per_head):
        flat = per_head.reshape(request_count, query_heads)
        return jnp.repeat(flat, parts_per_head, axis=1).T[:, :, None]

    pieces = block_out.reshape(request_count, ctx_count, column_width).transpose(1, 0, 2)
    packed = jnp.concatenate([pieces, by_owner(block_max), by_owner(block_sum)], axis=2)
    packed = lax.all_to_all(packed, "ctx", 0, 0, tiled=True)
    span_out = packed[:, :, :column_width]
    span_max = packed[:, :, column_width]
    span_sum = packed[:, :, column_width + 1]
    own_score = lax.dynamic_index_in_dim(by_owner(new_score), ctx_index, 0, keepdims=False)[:, 0]
    own_value = lax.dynamic_slice_in_dim(
        fresh_value.reshape(request_count, HEAD_SIZE),
        (ctx_index % parts_per_head) * column_width,
        column_width,
        1,
    ).astype(jnp.float32)
    peak = jnp.maximum(jnp.max(span_max, axis=0), own_score)
    factor = jnp.exp(span_max - peak)
    new_factor = jnp.exp(own_score - peak)
    total_sum = jnp.sum(span_sum * factor, axis=0) + new_factor
    merged = jnp.sum(span_out * factor[..., None], axis=0) + new_factor[:, None] * own_value
    own_columns = (merged / total_sum[:, None]).astype(jnp.bfloat16)
    partial_out = jnp.dot(own_columns, w_out[0], preferred_element_type=jnp.float32)
    width_dev = hidden.shape[1]
    pieces = (
        partial_out.astype(jnp.bfloat16)
        .reshape(request_count, ctx_count, width_dev)
        .transpose(1, 0, 2)
    )
    tp_count = lax.axis_size("tp")
    pieces = jnp.broadcast_to(pieces[None], (tp_count,) + pieces.shape).reshape(
        tp_count * ctx_count, request_count, width_dev
    )
    pieces = lax.all_to_all(pieces, ("tp", "ctx"), 0, 0, tiled=True)
    branch_out = pieces.astype(jnp.float32).sum(axis=0)
    section_rows = (hidden_f + branch_out).astype(jnp.bfloat16)
    arrived = from_behind(section_rows, "section", 1)
    selector = (routing[0][:, None] == jnp.arange(request_count, dtype=jnp.int32)[None, :]).astype(
        jnp.bfloat16
    )
    handed = jnp.dot(selector, arrived, preferred_element_type=jnp.float32).astype(jnp.bfloat16)
    return (handed, branch_out)


def solution(mesh):
    return jax.shard_map(
        per_device,
        mesh=mesh,
        in_specs=(
            P("section", "ctx"),
            P("section", "ctx"),
            P("section", "ctx", "tp"),
            P("section", "ctx", "tp"),
            P("section", "ctx", "tp"),
            P("section", ("tp", "ctx"), None),
            P("section", "ctx", "tp"),
            P("section", "ctx", "tp"),
            P("section"),
            P("section", "ctx", None),
            P("section", None),
        ),
        out_specs=(P("section", "ctx"), P("section", "ctx")),
        check_vma=False,
    )
```

```python
import functools

import jax
import jax.numpy as jnp
import numpy as np
from jax import lax
from jax.experimental import pallas as pl
from jax.experimental.pallas import tpu as pltpu
from jax.sharding import PartitionSpec as P

HEAD_SIZE = 128
EPSILON = 1e-05
NEGATIVE = -1e30
ROPE_BASE = 500000.0
CTX = ("x", "core")
SCALE = HEAD_SIZE ** (-0.5)
PROJECT_INPUTS = (
    "lengths",
    "plan",
    "frequency",
    "hidden",
    "gain",
    "w_query",
    "w_key",
    "w_value",
    "keys",
    "values",
    "w_out",
)
PROJECT_OUTPUTS = ("parts", "table", "hidden", "keys", "values", "w_out")
F32 = jnp.float32
BF16 = jnp.bfloat16


def whole(memory_space=pltpu.VMEM):
    return pl.BlockSpec(memory_space=memory_space)


def in_vmem(value):
    return pltpu.with_memory_space_constraint(value, pltpu.VMEM)


def project(*refs):
    count = len(PROJECT_INPUTS)
    sources = dict(zip(PROJECT_INPUTS, refs))
    outputs = dict(zip(PROJECT_OUTPUTS, refs[count:]))
    scratch = refs[count + len(PROJECT_OUTPUTS) :]
    held = dict(zip(PROJECT_INPUTS, scratch))
    held.update(keys=outputs["keys"], values=outputs["values"], w_out=outputs["w_out"])
    semaphores = scratch[-1]
    copies = {
        name: pltpu.make_async_copy(sources[name], held[name], semaphores.at[at])
        for at, name in enumerate(PROJECT_INPUTS)
    }
    for name in PROJECT_INPUTS:
        copies[name].start()

    out_ref, table_ref = outputs["parts"], outputs["table"]
    for name in ("lengths", "plan", "frequency"):
        copies[name].wait()
    lengths_ref, plan_ref = held["lengths"], held["plan"]
    requests = lengths_ref.shape[0]
    row = lax.broadcasted_iota(jnp.int32, (requests, HEAD_SIZE), 0)
    lane = lax.broadcasted_iota(jnp.int32, (requests, HEAD_SIZE), 1)
    length = jnp.zeros((requests, HEAD_SIZE), jnp.int32)
    live = jnp.zeros((requests, HEAD_SIZE), jnp.int32)
    for request in range(requests):
        length = jnp.where(row == request, lengths_ref[request], length)
        live = jnp.where(row == request, plan_ref[0, 1, request] - plan_ref[0, 0, request], live)
    angles = length.astype(F32) * held["frequency"][...]
    sine = jnp.sin(angles)
    table_ref[:, :HEAD_SIZE] = jnp.cos(angles)
    table_ref[:, HEAD_SIZE : 2 * HEAD_SIZE] = jnp.where(lane < HEAD_SIZE // 2, -sine, sine)
    table_ref[:, 2 * HEAD_SIZE :] = live.astype(F32)

    for name in ("hidden", "gain"):
        copies[name].wait()
    hidden = held["hidden"][...].astype(F32)
    outputs["hidden"][...] = hidden
    scaled = (hidden * held["gain"][...]).astype(BF16)
    squares = jnp.sum(hidden * hidden, axis=1, keepdims=True)
    squares = jnp.broadcast_to(squares, (requests, HEAD_SIZE))
    at = 0
    for name in ("w_query", "w_key", "w_value"):
        copies[name].wait()
        part = jnp.dot(scaled, held[name][0], preferred_element_type=F32)
        width = part.shape[1]
        for peer in range(out_ref.shape[0]):
            out_ref[peer, :, at : at + width] = part
        at += width
    for peer in range(out_ref.shape[0]):
        out_ref[peer, :, at:] = squares
    for name in ("keys", "values", "w_out"):
        copies[name].wait()


def attend(model_width, parts_ref, table_ref, keys_ref, values_ref, out_ref):
    total = parts_ref[0]
    for peer in range(1, parts_ref.shape[0]):
        total = total + parts_ref[peer]
    requests, heads = keys_ref.shape[0], 4
    rows = heads * requests
    slots = keys_ref.shape[1]
    squares = total[:, 6 * HEAD_SIZE : 6 * HEAD_SIZE + 1]
    inverse = lax.rsqrt(squares / model_width + EPSILON)
    cosine = table_ref[:, :HEAD_SIZE]
    sine = table_ref[:, HEAD_SIZE : 2 * HEAD_SIZE]

    def rotated(at):
        part = total[:, at * HEAD_SIZE : (at + 1) * HEAD_SIZE] * inverse
        return part * cosine + pltpu.roll(part, HEAD_SIZE // 2, 1) * sine

    query = jnp.concatenate([rotated(head) for head in range(heads)], axis=0).astype(BF16)
    new_key = rotated(heads).astype(BF16).astype(F32)
    new_value = total[:, 5 * HEAD_SIZE : 6 * HEAD_SIZE] * inverse
    new_value = new_value.astype(BF16).astype(F32)
    request_of_row = lax.broadcasted_iota(jnp.int32, (rows, 1), 0) % requests

    scores = jnp.zeros((rows, slots), F32)
    for request in range(requests):
        own = lax.dot_general(
            query, keys_ref[request], (((1,), (1,)), ((), ())), preferred_element_type=F32
        )
        scores = jnp.where(request_of_row == request, own, scores)
    counts = jnp.concatenate([table_ref[:, 2 * HEAD_SIZE : 2 * HEAD_SIZE + 1]] * heads, axis=0)
    slot = lax.broadcasted_iota(jnp.int32, (rows, slots), 1)
    live = slot < counts.astype(jnp.int32)
    scores = jnp.where(live, scores * SCALE, NEGATIVE)
    block_max = jnp.max(scores, axis=1, keepdims=True)
    weights = jnp.where(live, jnp.exp(scores - block_max), 0.0)
    block_sum = jnp.sum(weights, axis=1, keepdims=True)
    weights = weights.astype(BF16)
    block_out = jnp.zeros((rows, HEAD_SIZE), F32)
    for request in range(requests):
        own = jnp.dot(weights, values_ref[request], preferred_element_type=F32)
        block_out = jnp.where(request_of_row == request, own, block_out)

    new_key = jnp.concatenate([new_key] * heads, axis=0)
    new_value = jnp.concatenate([new_value] * heads, axis=0)
    new_score = jnp.sum(query.astype(F32) * new_key, axis=1, keepdims=True) * SCALE
    takes_new = (lax.axis_index("x") == 0) & (lax.axis_index("core") == 0)
    peak = jnp.where(takes_new, jnp.maximum(block_max, new_score), block_max)
    factor = jnp.exp(block_max - peak)
    new_factor = jnp.where(takes_new, jnp.exp(new_score - peak), 0.0)
    block_sum = block_sum * factor + new_factor
    block_out = block_out * factor + new_factor * new_value

    lane = lax.broadcasted_iota(jnp.int32, (rows, HEAD_SIZE), 1)
    half = HEAD_SIZE // 2
    statistics = jnp.where(lane == half, peak, block_sum)
    lower = jnp.where(lane < half, block_out, statistics)
    upper = jnp.where(lane < half, pltpu.roll(block_out, half, 1), statistics)
    for head in range(heads):
        own = slice(head * requests, (head + 1) * requests)
        out_ref[2 * head] = lower[own]
        out_ref[2 * head + 1] = upper[own]


def merge_and_project(parts_ref, w_ref, out_ref):
    half = HEAD_SIZE // 2
    parts = parts_ref[...]
    span_max = parts[:, :, half : half + 1]
    peak = jnp.max(span_max, axis=0, keepdims=True)
    merged = jnp.sum(parts * jnp.exp(span_max - peak), axis=0)
    attended = (merged / merged[:, half + 1 : half + 2])[:, :half].astype(BF16)
    result = jnp.dot(attended, w_ref[0], preferred_element_type=F32).astype(BF16)
    peers, width = out_ref.shape[0], out_ref.shape[2]
    columns = result.shape[1] // width
    for peer in range(peers):
        at = peer % columns * width
        out_ref[peer] = result[:, at : at + width]


def from_behind(value, axis, steps):
    count = lax.axis_size(axis)
    return lax.ppermute(value, axis, [(source, (source + steps) % count) for source in range(count)])


def frequencies():
    half_dim = HEAD_SIZE // 2
    frequency = ROPE_BASE ** (-2.0 * np.arange(half_dim) / HEAD_SIZE)
    return np.concatenate([frequency, frequency])[None, :].astype(np.float32)


def per_device(
    hidden,
    gain,
    w_query,
    key_weight,
    value_weight,
    w_out,
    key_cache_slots,
    value_cache_slots,
    lengths,
    plan,
    routing,
):
    requests, width = hidden.shape
    ctx_count = lax.axis_size(CTX)
    packed_width = w_query.shape[2] + 2 * key_weight.shape[2] + HEAD_SIZE
    sources = (
        lengths,
        jnp.transpose(plan, (1, 2, 0)),
        jnp.asarray(frequencies()),
        hidden,
        gain,
        w_query,
        key_weight,
        value_weight,
        key_cache_slots,
        value_cache_slots,
        w_out,
    )
    moved = sources[-3:]
    parts, table, hidden_f, keys, values, w_out = pl.pallas_call(
        project,
        out_shape=(
            pltpu.VMEM((ctx_count, requests, packed_width), F32),
            pltpu.VMEM((requests, 3 * HEAD_SIZE), F32),
            pltpu.VMEM((requests, width), F32),
        )
        + tuple(pltpu.VMEM(source.shape, source.dtype) for source in moved),
        in_specs=[whole(pltpu.HBM)] * len(sources),
        out_specs=(whole(),) * 6,
        scratch_shapes=[
            (pltpu.SMEM if source.dtype == jnp.int32 else pltpu.VMEM)(source.shape, source.dtype)
            for source in sources[:-3]
        ]
        + [pltpu.SemaphoreType.DMA((len(sources),))],
        name="project",
        compiler_params=pltpu.CompilerParams(vmem_limit_bytes=16 * 2**20),
    )(*[pltpu.with_memory_space_constraint(source, pltpu.HBM) for source in sources])
    parts = lax.all_to_all(parts, CTX, 0, 0, tiled=True)
    spans = pl.pallas_call(
        functools.partial(attend, width * ctx_count),
        out_shape=pltpu.VMEM((ctx_count, requests, HEAD_SIZE), F32),
        in_specs=[whole()] * 4,
        out_specs=whole(),
        name="attend",
        compiler_params=pltpu.CompilerParams(vmem_limit_bytes=16 * 2**20),
    )(parts, table, in_vmem(keys), in_vmem(values))
    spans = lax.all_to_all(spans, CTX, 0, 0, tiled=True)
    pieces = pl.pallas_call(
        merge_and_project,
        out_shape=pltpu.VMEM((lax.axis_size("tp") * ctx_count, requests, width), BF16),
        in_specs=[whole()] * 2,
        out_specs=whole(),
        name="merge_and_project",
    )(spans, in_vmem(w_out))
    pieces = lax.all_to_all(pieces, ("tp",) + CTX, 0, 0, tiled=True)
    section_rows = (hidden_f + pieces.astype(F32).sum(axis=0)).astype(BF16)
    section_rows, pieces = lax.optimization_barrier((section_rows, pieces))
    arrived = from_behind(section_rows, "section", 1)
    branch_out = pieces.astype(F32).sum(axis=0)
    selector = (routing[0][:, None] == jnp.arange(requests, dtype=jnp.int32)[None, :]).astype(BF16)
    handed = jnp.dot(selector, arrived, preferred_element_type=F32).astype(BF16)
    return (handed, branch_out)


def solution(mesh):
    sizes = mesh.shape
    devices = mesh.devices.reshape(sizes["section"], sizes["tp"], sizes["ctx"] // 2, 2)
    mesh = jax.sharding.Mesh(devices, ("section", "tp", "x", "core"))
    return jax.shard_map(
        per_device,
        mesh=mesh,
        in_specs=(
            P("section", CTX),
            P("section", CTX),
            P("section", CTX, "tp"),
            P("section", CTX, "tp"),
            P("section", CTX, "tp"),
            P("section", ("tp",) + CTX, None),
            P("section", CTX, "tp"),
            P("section", CTX, "tp"),
            P("section"),
            P("section", CTX, None),
            P("section", None),
        ),
        out_specs=(P("section", CTX), P("section", CTX)),
        check_vma=False,
    )
```

```python
import functools

import jax
import jax.numpy as jnp
import numpy as np
from jax import lax
from jax.experimental import pallas as pl
from jax.experimental.pallas import tpu as pltpu
from jax.sharding import PartitionSpec as P

HEAD_SIZE = 128
EPSILON = 1e-05
NEGATIVE = -1e30
ROPE_BASE = 500000.0
CTX = ("far", "near", "core")
LAST = ("tp", "near", "core")
SCALE = HEAD_SIZE ** (-0.5)
PROJECT_INPUTS = (
    "lengths",
    "plan",
    "frequency",
    "hidden",
    "gain",
    "w_query",
    "w_key",
    "w_value",
    "keys",
    "values",
    "w_out",
)
PROJECT_OUTPUTS = ("parts", "table", "hidden", "keys", "values", "w_out")
F32 = jnp.float32
BF16 = jnp.bfloat16


def whole(memory_space=pltpu.VMEM):
    return pl.BlockSpec(memory_space=memory_space)


def in_vmem(value):
    return pltpu.with_memory_space_constraint(value, pltpu.VMEM)


def project(*refs):
    count = len(PROJECT_INPUTS)
    sources = dict(zip(PROJECT_INPUTS, refs))
    outputs = dict(zip(PROJECT_OUTPUTS, refs[count:]))
    scratch = refs[count + len(PROJECT_OUTPUTS) :]
    held = dict(zip(PROJECT_INPUTS, scratch))
    held.update(keys=outputs["keys"], values=outputs["values"], w_out=outputs["w_out"])
    semaphores = scratch[-1]
    copies = {
        name: pltpu.make_async_copy(sources[name], held[name], semaphores.at[at])
        for at, name in enumerate(PROJECT_INPUTS)
    }
    for name in PROJECT_INPUTS:
        copies[name].start()

    out_ref, table_ref = outputs["parts"], outputs["table"]
    for name in ("lengths", "plan", "frequency"):
        copies[name].wait()
    lengths_ref, plan_ref = held["lengths"], held["plan"]
    requests = lengths_ref.shape[0]
    row = lax.broadcasted_iota(jnp.int32, (requests, HEAD_SIZE), 0)
    lane = lax.broadcasted_iota(jnp.int32, (requests, HEAD_SIZE), 1)
    length = jnp.zeros((requests, HEAD_SIZE), jnp.int32)
    live = jnp.zeros((requests, HEAD_SIZE), jnp.int32)
    for request in range(requests):
        length = jnp.where(row == request, lengths_ref[request], length)
        live = jnp.where(row == request, plan_ref[0, 1, request] - plan_ref[0, 0, request], live)
    angles = length.astype(F32) * held["frequency"][...]
    sine = jnp.sin(angles)
    table_ref[:, :HEAD_SIZE] = jnp.cos(angles)
    table_ref[:, HEAD_SIZE : 2 * HEAD_SIZE] = jnp.where(lane < HEAD_SIZE // 2, -sine, sine)
    table_ref[:, 2 * HEAD_SIZE :] = live.astype(F32)

    for name in ("hidden", "gain"):
        copies[name].wait()
    hidden = held["hidden"][...].astype(F32)
    outputs["hidden"][...] = hidden
    scaled = (hidden * held["gain"][...]).astype(BF16)
    squares = jnp.sum(hidden * hidden, axis=1, keepdims=True)
    squares = jnp.broadcast_to(squares, (requests, HEAD_SIZE))
    at = 0
    for name in ("w_query", "w_key", "w_value"):
        copies[name].wait()
        part = jnp.dot(scaled, held[name][0], preferred_element_type=F32)
        width = part.shape[1]
        for peer in range(out_ref.shape[0]):
            out_ref[peer, :, at : at + width] = part
        at += width
    for peer in range(out_ref.shape[0]):
        out_ref[peer, :, at:] = squares
    for name in ("keys", "values", "w_out"):
        copies[name].wait()


def attend(model_width, parts_ref, table_ref, keys_ref, values_ref, out_ref):
    total = parts_ref[0]
    for peer in range(1, parts_ref.shape[0]):
        total = total + parts_ref[peer]
    requests, heads = keys_ref.shape[0], 4
    rows = heads * requests
    slots = keys_ref.shape[1]
    squares = total[:, 6 * HEAD_SIZE : 6 * HEAD_SIZE + 1]
    inverse = lax.rsqrt(squares / model_width + EPSILON)
    cosine = table_ref[:, :HEAD_SIZE]
    sine = table_ref[:, HEAD_SIZE : 2 * HEAD_SIZE]

    def rotated(at):
        part = total[:, at * HEAD_SIZE : (at + 1) * HEAD_SIZE] * inverse
        return part * cosine + pltpu.roll(part, HEAD_SIZE // 2, 1) * sine

    query = jnp.concatenate([rotated(head) for head in range(heads)], axis=0).astype(BF16)
    new_key = rotated(heads).astype(BF16).astype(F32)
    new_value = total[:, 5 * HEAD_SIZE : 6 * HEAD_SIZE] * inverse
    new_value = new_value.astype(BF16).astype(F32)
    request_of_row = lax.broadcasted_iota(jnp.int32, (rows, 1), 0) % requests

    scores = jnp.zeros((rows, slots), F32)
    for request in range(requests):
        own = lax.dot_general(
            query, keys_ref[request], (((1,), (1,)), ((), ())), preferred_element_type=F32
        )
        scores = jnp.where(request_of_row == request, own, scores)
    counts = jnp.concatenate([table_ref[:, 2 * HEAD_SIZE : 2 * HEAD_SIZE + 1]] * heads, axis=0)
    slot = lax.broadcasted_iota(jnp.int32, (rows, slots), 1)
    live = slot < counts.astype(jnp.int32)
    scores = jnp.where(live, scores * SCALE, NEGATIVE)
    block_max = jnp.max(scores, axis=1, keepdims=True)
    weights = jnp.where(live, jnp.exp(scores - block_max), 0.0)
    block_sum = jnp.sum(weights, axis=1, keepdims=True)
    weights = weights.astype(BF16)
    block_out = jnp.zeros((rows, HEAD_SIZE), F32)
    for request in range(requests):
        own = jnp.dot(weights, values_ref[request], preferred_element_type=F32)
        block_out = jnp.where(request_of_row == request, own, block_out)

    new_key = jnp.concatenate([new_key] * heads, axis=0)
    new_value = jnp.concatenate([new_value] * heads, axis=0)
    new_score = jnp.sum(query.astype(F32) * new_key, axis=1, keepdims=True) * SCALE
    takes_new = lax.axis_index(CTX) == 0
    peak = jnp.where(takes_new, jnp.maximum(block_max, new_score), block_max)
    factor = jnp.exp(block_max - peak)
    new_factor = jnp.where(takes_new, jnp.exp(new_score - peak), 0.0)
    block_sum = block_sum * factor + new_factor
    block_out = block_out * factor + new_factor * new_value

    lane = lax.broadcasted_iota(jnp.int32, (rows, HEAD_SIZE), 1)
    half = HEAD_SIZE // 2
    statistics = jnp.where(lane == half, peak, block_sum)
    lower = jnp.where(lane < half, block_out, statistics)
    upper = jnp.where(lane < half, pltpu.roll(block_out, half, 1), statistics)
    for head in range(heads):
        for place, source in enumerate((head, head ^ 2)):
            rows_of = slice(source * requests, (source + 1) * requests)
            to = slice(place * requests, (place + 1) * requests)
            out_ref[2 * head, to] = lower[rows_of]
            out_ref[2 * head + 1, to] = upper[rows_of]


def merge_and_project(parts_ref, kept_ref, swapped_ref, out_ref):
    half = HEAD_SIZE // 2
    parts = parts_ref[...]
    span_max = parts[:, :, half : half + 1]
    peak = jnp.max(span_max, axis=0, keepdims=True)
    merged = jnp.sum(parts * jnp.exp(span_max - peak), axis=0)
    attended = merged / merged[:, half + 1 : half + 2]
    peers, requests, width = out_ref.shape
    own = attended[:requests, :half].astype(BF16)
    far = attended[requests:, :half].astype(BF16)
    result = jnp.dot(own, kept_ref[...], preferred_element_type=F32)
    result += jnp.dot(far, swapped_ref[...], preferred_element_type=F32)
    result = result.astype(BF16)
    columns = result.shape[1] // width
    for peer in range(peers):
        at = peer % columns * width
        out_ref[peer] = result[:, at : at + width]


def from_behind(value, axis, steps):
    count = lax.axis_size(axis)
    return lax.ppermute(value, axis, [(source, (source + steps) % count) for source in range(count)])


def frequencies():
    half_dim = HEAD_SIZE // 2
    frequency = ROPE_BASE ** (-2.0 * np.arange(half_dim) / HEAD_SIZE)
    return np.concatenate([frequency, frequency])[None, :].astype(np.float32)


def per_device(
    hidden,
    gain,
    w_query,
    key_weight,
    value_weight,
    w_out,
    key_cache_slots,
    value_cache_slots,
    lengths,
    plan,
    routing,
):
    requests, width = hidden.shape
    ctx_count = lax.axis_size(CTX)
    packed_width = w_query.shape[2] + 2 * key_weight.shape[2] + HEAD_SIZE
    sources = (
        lengths,
        jnp.transpose(plan, (1, 2, 0)),
        jnp.asarray(frequencies()),
        hidden,
        gain,
        w_query,
        key_weight,
        value_weight,
        key_cache_slots,
        value_cache_slots,
        w_out,
    )
    moved = sources[-3:]
    parts, table, hidden_f, keys, values, w_out = pl.pallas_call(
        project,
        out_shape=(
            pltpu.VMEM((ctx_count, requests, packed_width), F32),
            pltpu.VMEM((requests, 3 * HEAD_SIZE), F32),
            pltpu.VMEM((requests, width), F32),
        )
        + tuple(pltpu.VMEM(source.shape, source.dtype) for source in moved),
        in_specs=[whole(pltpu.HBM)] * len(sources),
        out_specs=(whole(),) * 6,
        scratch_shapes=[
            (pltpu.SMEM if source.dtype == jnp.int32 else pltpu.VMEM)(source.shape, source.dtype)
            for source in sources[:-3]
        ]
        + [pltpu.SemaphoreType.DMA((len(sources),))],
        name="project",
        compiler_params=pltpu.CompilerParams(vmem_limit_bytes=16 * 2**20),
    )(*[pltpu.with_memory_space_constraint(source, pltpu.HBM) for source in sources])
    parts, w_rows = lax.optimization_barrier((parts, w_out[0]))
    half_columns = w_rows.shape[1] // 2
    far = lax.axis_index("far")
    w_kept = lax.dynamic_slice_in_dim(w_rows, far * half_columns, half_columns, 1)
    w_sent = lax.dynamic_slice_in_dim(w_rows, (1 - far) * half_columns, half_columns, 1)
    w_swapped = from_behind(w_sent, "far", 1)
    parts = lax.all_to_all(parts, CTX, 0, 0, tiled=True)
    spans = pl.pallas_call(
        functools.partial(attend, width * ctx_count),
        out_shape=pltpu.VMEM((ctx_count, 2 * requests, HEAD_SIZE), F32),
        in_specs=[whole()] * 4,
        out_specs=whole(),
        name="attend",
        compiler_params=pltpu.CompilerParams(vmem_limit_bytes=16 * 2**20),
    )(in_vmem(parts), in_vmem(table), in_vmem(keys), in_vmem(values))
    spans = lax.all_to_all(spans, CTX, 0, 0, tiled=True)
    pieces = pl.pallas_call(
        merge_and_project,
        out_shape=pltpu.VMEM((lax.axis_size(LAST), requests, width), BF16),
        in_specs=[whole()] * 3,
        out_specs=whole(),
        name="merge_and_project",
    )(in_vmem(spans), in_vmem(w_kept), in_vmem(w_swapped))
    pieces = lax.all_to_all(pieces, LAST, 0, 0, tiled=True)
    section_rows = (hidden_f + pieces.astype(F32).sum(axis=0)).astype(BF16)
    section_rows, pieces = lax.optimization_barrier((section_rows, pieces))
    arrived = from_behind(section_rows, "section", 1)
    branch_out = pieces.astype(F32).sum(axis=0)
    selector = (routing[0][:, None] == jnp.arange(requests, dtype=jnp.int32)[None, :]).astype(BF16)
    handed = jnp.dot(selector, arrived, preferred_element_type=F32).astype(BF16)
    return (handed, branch_out)


def solution(mesh):
    sizes = mesh.shape
    devices = mesh.devices.reshape(sizes["section"], sizes["tp"], 2, 2, 2)
    mesh = jax.sharding.Mesh(devices, ("section", "tp") + CTX)
    return jax.shard_map(
        per_device,
        mesh=mesh,
        in_specs=(
            P("section", CTX),
            P("section", CTX),
            P("section", CTX, "tp"),
            P("section", CTX, "tp"),
            P("section", CTX, "tp"),
            P("section", ("tp",) + CTX, None),
            P("section", CTX, "tp"),
            P("section", CTX, "tp"),
            P("section"),
            P("section", CTX, None),
            P("section", None),
        ),
        out_specs=(P("section", CTX), P("section", CTX)),
        check_vma=False,
    )
```

```python
import functools

import jax
import jax.numpy as jnp
import numpy as np
from jax import lax
from jax.experimental import pallas as pl
from jax.experimental.pallas import tpu as pltpu
from jax.sharding import PartitionSpec as P

HEAD_SIZE = 128
EPSILON = 1e-05
NEGATIVE = -1e30
ROPE_BASE = 500000.0
CTX = ("far", "near", "core")
LAST = ("tp", "near", "core")
SCALE = HEAD_SIZE ** (-0.5)
F32 = jnp.float32
BF16 = jnp.bfloat16


def whole(memory_space=pltpu.VMEM):
    return pl.BlockSpec(memory_space=memory_space)


def in_vmem(value):
    return pltpu.with_memory_space_constraint(value, pltpu.VMEM)


def project(
    lengths_ref, plan_ref, frequency_ref, hidden_ref, gain_ref, query_ref, key_ref, value_ref,
    out_ref, table_ref, hidden_out_ref,
):
    hidden = hidden_ref[...].astype(F32)
    requests = hidden.shape[0]
    hidden_out_ref[...] = hidden
    scaled = (hidden * gain_ref[...]).astype(BF16)
    squares = jnp.sum(hidden * hidden, axis=1, keepdims=True)
    squares = jnp.broadcast_to(squares, (requests, HEAD_SIZE))
    at = 0
    for ref in (query_ref, key_ref, value_ref):
        part = jnp.dot(scaled, ref[0], preferred_element_type=F32)
        width = part.shape[1]
        for peer in range(out_ref.shape[0]):
            out_ref[peer, :, at : at + width] = part
        at += width
    for peer in range(out_ref.shape[0]):
        out_ref[peer, :, at:] = squares

    row = lax.broadcasted_iota(jnp.int32, (requests, HEAD_SIZE), 0)
    lane = lax.broadcasted_iota(jnp.int32, (requests, HEAD_SIZE), 1)
    length = jnp.zeros((requests, HEAD_SIZE), jnp.int32)
    live = jnp.zeros((requests, HEAD_SIZE), jnp.int32)
    for request in range(requests):
        length = jnp.where(row == request, lengths_ref[request], length)
        live = jnp.where(row == request, plan_ref[0, 1, request] - plan_ref[0, 0, request], live)
    angles = length.astype(F32) * frequency_ref[...]
    sine = jnp.sin(angles)
    table_ref[:, :HEAD_SIZE] = jnp.cos(angles)
    table_ref[:, HEAD_SIZE : 2 * HEAD_SIZE] = jnp.where(lane < HEAD_SIZE // 2, -sine, sine)
    table_ref[:, 2 * HEAD_SIZE :] = live.astype(F32)


def attend(model_width, parts_ref, table_ref, keys_ref, values_ref, out_ref):
    total = parts_ref[0]
    for peer in range(1, parts_ref.shape[0]):
        total = total + parts_ref[peer]
    requests, heads = keys_ref.shape[0], 4
    rows = heads * requests
    slots = keys_ref.shape[1]
    squares = total[:, 6 * HEAD_SIZE : 6 * HEAD_SIZE + 1]
    inverse = lax.rsqrt(squares / model_width + EPSILON)
    cosine = table_ref[:, :HEAD_SIZE]
    sine = table_ref[:, HEAD_SIZE : 2 * HEAD_SIZE]

    def rotated(at):
        part = total[:, at * HEAD_SIZE : (at + 1) * HEAD_SIZE] * inverse
        return part * cosine + pltpu.roll(part, HEAD_SIZE // 2, 1) * sine

    query = jnp.concatenate([rotated(head) for head in range(heads)], axis=0).astype(BF16)
    new_key = rotated(heads).astype(BF16).astype(F32)
    new_value = total[:, 5 * HEAD_SIZE : 6 * HEAD_SIZE] * inverse
    new_value = new_value.astype(BF16).astype(F32)
    request_of_row = lax.broadcasted_iota(jnp.int32, (rows, 1), 0) % requests

    scores = jnp.zeros((rows, slots), F32)
    for request in range(requests):
        own = lax.dot_general(
            query, keys_ref[request], (((1,), (1,)), ((), ())), preferred_element_type=F32
        )
        scores = jnp.where(request_of_row == request, own, scores)
    counts = jnp.concatenate([table_ref[:, 2 * HEAD_SIZE : 2 * HEAD_SIZE + 1]] * heads, axis=0)
    slot = lax.broadcasted_iota(jnp.int32, (rows, slots), 1)
    live = slot < counts.astype(jnp.int32)
    scores = jnp.where(live, scores * SCALE, NEGATIVE)
    block_max = jnp.max(scores, axis=1, keepdims=True)
    weights = jnp.where(live, jnp.exp(scores - block_max), 0.0)
    block_sum = jnp.sum(weights, axis=1, keepdims=True)
    weights = weights.astype(BF16)
    block_out = jnp.zeros((rows, HEAD_SIZE), F32)
    for request in range(requests):
        own = jnp.dot(weights, values_ref[request], preferred_element_type=F32)
        block_out = jnp.where(request_of_row == request, own, block_out)

    new_key = jnp.concatenate([new_key] * heads, axis=0)
    new_value = jnp.concatenate([new_value] * heads, axis=0)
    new_score = jnp.sum(query.astype(F32) * new_key, axis=1, keepdims=True) * SCALE
    takes_new = lax.axis_index(CTX) == 0
    peak = jnp.where(takes_new, jnp.maximum(block_max, new_score), block_max)
    factor = jnp.exp(block_max - peak)
    new_factor = jnp.where(takes_new, jnp.exp(new_score - peak), 0.0)
    block_sum = block_sum * factor + new_factor
    block_out = block_out * factor + new_factor * new_value

    lane = lax.broadcasted_iota(jnp.int32, (rows, HEAD_SIZE), 1)
    half = HEAD_SIZE // 2
    statistics = jnp.where(lane == half, peak, block_sum)
    lower = jnp.where(lane < half, block_out, statistics)
    upper = jnp.where(lane < half, pltpu.roll(block_out, half, 1), statistics)
    for head in range(heads):
        for place, source in enumerate((head, head ^ 2)):
            rows_of = slice(source * requests, (source + 1) * requests)
            to = slice(place * requests, (place + 1) * requests)
            out_ref[2 * head, to] = lower[rows_of]
            out_ref[2 * head + 1, to] = upper[rows_of]


def merge_and_project(parts_ref, kept_ref, swapped_ref, out_ref):
    half = HEAD_SIZE // 2
    parts = parts_ref[...]
    span_max = parts[:, :, half : half + 1]
    peak = jnp.max(span_max, axis=0, keepdims=True)
    merged = jnp.sum(parts * jnp.exp(span_max - peak), axis=0)
    attended = merged / merged[:, half + 1 : half + 2]
    peers, requests, width = out_ref.shape
    own = attended[:requests, :half].astype(BF16)
    far = attended[requests:, :half].astype(BF16)
    result = jnp.dot(own, kept_ref[...], preferred_element_type=F32)
    result += jnp.dot(far, swapped_ref[...], preferred_element_type=F32)
    result = result.astype(BF16)
    columns = result.shape[1] // width
    for peer in range(peers):
        at = peer % columns * width
        out_ref[peer] = result[:, at : at + width]


def from_behind(value, axis, steps):
    count = lax.axis_size(axis)
    return lax.ppermute(value, axis, [(source, (source + steps) % count) for source in range(count)])


def frequencies():
    half_dim = HEAD_SIZE // 2
    frequency = ROPE_BASE ** (-2.0 * np.arange(half_dim) / HEAD_SIZE)
    return np.concatenate([frequency, frequency])[None, :].astype(np.float32)


def per_device(
    hidden,
    gain,
    w_query,
    key_weight,
    value_weight,
    w_out,
    key_cache_slots,
    value_cache_slots,
    lengths,
    plan,
    routing,
):
    requests, width = hidden.shape
    ctx_count = lax.axis_size(CTX)
    packed_width = w_query.shape[2] + 2 * key_weight.shape[2] + HEAD_SIZE
    w_rows = w_out[0]
    half_columns = w_rows.shape[1] // 2
    far = lax.axis_index("far")
    w_kept = lax.dynamic_slice_in_dim(w_rows, far * half_columns, half_columns, 1)
    w_sent = lax.dynamic_slice_in_dim(w_rows, (1 - far) * half_columns, half_columns, 1)
    hidden, w_sent = lax.optimization_barrier((hidden, w_sent))
    w_swapped = from_behind(w_sent, "far", 1)
    sources = (
        lengths,
        jnp.transpose(plan, (1, 2, 0)),
        jnp.asarray(frequencies()),
        hidden,
        gain,
        w_query,
        key_weight,
        value_weight,
    )
    parts, table, hidden_f = pl.pallas_call(
        project,
        out_shape=(
            pltpu.VMEM((ctx_count, requests, packed_width), F32),
            pltpu.VMEM((requests, 3 * HEAD_SIZE), F32),
            pltpu.VMEM((requests, width), F32),
        ),
        in_specs=[whole(pltpu.SMEM)] * 2 + [whole()] * 6,
        out_specs=(whole(),) * 3,
        name="project",
    )(*sources)
    parts = lax.all_to_all(parts, CTX, 0, 0, tiled=True)
    spans = pl.pallas_call(
        functools.partial(attend, width * ctx_count),
        out_shape=pltpu.VMEM((ctx_count, 2 * requests, HEAD_SIZE), F32),
        in_specs=[whole()] * 4,
        out_specs=whole(),
        name="attend",
        compiler_params=pltpu.CompilerParams(vmem_limit_bytes=16 * 2**20),
    )(in_vmem(parts), in_vmem(table), key_cache_slots, value_cache_slots)
    spans = lax.all_to_all(spans, CTX, 0, 0, tiled=True)
    pieces = pl.pallas_call(
        merge_and_project,
        out_shape=pltpu.VMEM((lax.axis_size(LAST), requests, width), BF16),
        in_specs=[whole()] * 3,
        out_specs=whole(),
        name="merge_and_project",
    )(in_vmem(spans), in_vmem(w_kept), in_vmem(w_swapped))
    pieces = lax.all_to_all(pieces, LAST, 0, 0, tiled=True)
    section_rows = (hidden_f + pieces.astype(F32).sum(axis=0)).astype(BF16)
    section_rows, pieces = lax.optimization_barrier((section_rows, pieces))
    arrived = from_behind(section_rows, "section", 1)
    branch_out = pieces.astype(F32).sum(axis=0)
    selector = (routing[0][:, None] == jnp.arange(requests, dtype=jnp.int32)[None, :]).astype(BF16)
    handed = jnp.dot(selector, arrived, preferred_element_type=F32).astype(BF16)
    return (handed, branch_out)


def solution(mesh):
    sizes = mesh.shape
    devices = mesh.devices.reshape(sizes["section"], sizes["tp"], 2, 2, 2)
    mesh = jax.sharding.Mesh(devices, ("section", "tp") + CTX)
    return jax.shard_map(
        per_device,
        mesh=mesh,
        in_specs=(
            P("section", CTX),
            P("section", CTX),
            P("section", CTX, "tp"),
            P("section", CTX, "tp"),
            P("section", CTX, "tp"),
            P("section", ("tp",) + CTX, None),
            P("section", CTX, "tp"),
            P("section", CTX, "tp"),
            P("section"),
            P("section", CTX, None),
            P("section", None),
        ),
        out_specs=(P("section", CTX), P("section", CTX)),
        check_vma=False,
    )
```

```python
import functools

import jax
import jax.numpy as jnp
import numpy as np
from jax import lax
from jax.experimental import pallas as pl
from jax.experimental.pallas import tpu as pltpu
from jax.sharding import PartitionSpec as P

HEAD_SIZE = 128
EPSILON = 1e-05
NEGATIVE = -1e30
ROPE_BASE = 500000.0
CTX = ("far", "near", "core")
LAST = ("tp", "far", "near")
CHIPS = 4
SCALE = HEAD_SIZE ** (-0.5)
FETCH_INPUTS = (
    "lengths",
    "plan",
    "frequency",
    "gain",
    "hidden",
    "w_query",
    "w_key",
    "w_value",
    "w_out",
)
FETCH_OUTPUTS = (
    "hidden",
    "scaled",
    "squares",
    "table",
    "w_query",
    "w_key",
    "w_value",
    "w_sent",
    "w_kept",
)
F32 = jnp.float32
BF16 = jnp.bfloat16


def whole(memory_space=pltpu.VMEM):
    return pl.BlockSpec(memory_space=memory_space)


def in_vmem(value):
    return pltpu.with_memory_space_constraint(value, pltpu.VMEM)


def fetch(*refs):
    count = len(FETCH_INPUTS)
    outputs = dict(zip(FETCH_OUTPUTS, refs[count:]))
    lengths_ref, plan_ref, frequency_ref, gain_ref, semaphores = refs[count + len(FETCH_OUTPUTS) :]
    held = dict(outputs, lengths=lengths_ref, plan=plan_ref, frequency=frequency_ref, gain=gain_ref)
    sources = dict(zip(FETCH_INPUTS, refs))
    w_ref = sources.pop("w_out")
    core, width = lax.axis_index("core"), outputs["w_kept"].shape[1] // CHIPS
    for name, whose in (("w_sent", 1 - core), ("w_kept", core)):
        for chip in range(CHIPS):
            start = pl.multiple_of((2 * chip + whose) * width, HEAD_SIZE)
            at = pl.ds(chip * width, width)
            sources[name, chip] = w_ref.at[0, :, pl.ds(start, width)]
            held[name, chip] = outputs[name].at[:, at]
    copies = {
        name: pltpu.make_async_copy(source, held[name], semaphores.at[at])
        for at, (name, source) in enumerate(sources.items())
    }
    for copy in copies.values():
        copy.start()

    for name in ("lengths", "plan", "frequency", "hidden", "gain"):
        copies[name].wait()
    hidden = held["hidden"][...].astype(F32)
    requests = hidden.shape[0]
    outputs["scaled"][...] = (hidden * gain_ref[...]).astype(BF16)
    squares = jnp.sum(hidden * hidden, axis=1, keepdims=True)
    outputs["squares"][...] = jnp.broadcast_to(squares, (requests, HEAD_SIZE))
    row = lax.broadcasted_iota(jnp.int32, (requests, HEAD_SIZE), 0)
    lane = lax.broadcasted_iota(jnp.int32, (requests, HEAD_SIZE), 1)
    length = jnp.zeros((requests, HEAD_SIZE), jnp.int32)
    live = jnp.zeros((requests, HEAD_SIZE), jnp.int32)
    for request in range(requests):
        length = jnp.where(row == request, lengths_ref[request], length)
        live = jnp.where(row == request, plan_ref[0, 1, request] - plan_ref[0, 0, request], live)
    angles = length.astype(F32) * frequency_ref[...]
    sine = jnp.sin(angles)
    table_ref = outputs["table"]
    table_ref[:, :HEAD_SIZE] = jnp.cos(angles)
    table_ref[:, HEAD_SIZE : 2 * HEAD_SIZE] = jnp.where(lane < HEAD_SIZE // 2, -sine, sine)
    table_ref[:, 2 * HEAD_SIZE :] = live.astype(F32)
    for name in ("w_query", "w_key", "w_value"):
        copies.pop(name).wait()
    for name in ("lengths", "plan", "frequency", "hidden", "gain"):
        copies.pop(name)
    for copy in copies.values():
        copy.wait()


def project(scaled_ref, squares_ref, query_ref, key_ref, value_ref, out_ref):
    scaled = scaled_ref[...]
    at = 0
    for ref in (query_ref, key_ref, value_ref):
        part = jnp.dot(scaled, ref[0], preferred_element_type=F32)
        width = part.shape[1]
        for peer in range(out_ref.shape[0]):
            out_ref[peer, :, at : at + width] = part
        at += width
    squares = squares_ref[...]
    for peer in range(out_ref.shape[0]):
        out_ref[peer, :, at:] = squares


def attend(model_width, parts_ref, table_ref, keys_ref, values_ref, out_ref):
    total = parts_ref[0]
    for peer in range(1, parts_ref.shape[0]):
        total = total + parts_ref[peer]
    requests, heads = keys_ref.shape[0], 4
    rows = heads * requests
    slots = keys_ref.shape[1]
    squares = total[:, 6 * HEAD_SIZE : 6 * HEAD_SIZE + 1]
    inverse = lax.rsqrt(squares / model_width + EPSILON)
    cosine = table_ref[:, :HEAD_SIZE]
    sine = table_ref[:, HEAD_SIZE : 2 * HEAD_SIZE]

    def rotated(at):
        part = total[:, at * HEAD_SIZE : (at + 1) * HEAD_SIZE] * inverse
        return part * cosine + pltpu.roll(part, HEAD_SIZE // 2, 1) * sine

    query = jnp.concatenate([rotated(head) for head in range(heads)], axis=0).astype(BF16)
    new_key = rotated(heads).astype(BF16).astype(F32)
    new_value = total[:, 5 * HEAD_SIZE : 6 * HEAD_SIZE] * inverse
    new_value = new_value.astype(BF16).astype(F32)
    request_of_row = lax.broadcasted_iota(jnp.int32, (rows, 1), 0) % requests

    scores = jnp.zeros((rows, slots), F32)
    for request in range(requests):
        own = lax.dot_general(
            query, keys_ref[request], (((1,), (1,)), ((), ())), preferred_element_type=F32
        )
        scores = jnp.where(request_of_row == request, own, scores)
    counts = jnp.concatenate([table_ref[:, 2 * HEAD_SIZE : 2 * HEAD_SIZE + 1]] * heads, axis=0)
    slot = lax.broadcasted_iota(jnp.int32, (rows, slots), 1)
    live = slot < counts.astype(jnp.int32)
    scores = jnp.where(live, scores * SCALE, NEGATIVE)
    block_max = jnp.max(scores, axis=1, keepdims=True)
    weights = jnp.where(live, jnp.exp(scores - block_max), 0.0)
    block_sum = jnp.sum(weights, axis=1, keepdims=True)
    weights = weights.astype(BF16)
    block_out = jnp.zeros((rows, HEAD_SIZE), F32)
    for request in range(requests):
        own = jnp.dot(weights, values_ref[request], preferred_element_type=F32)
        block_out = jnp.where(request_of_row == request, own, block_out)

    new_key = jnp.concatenate([new_key] * heads, axis=0)
    new_value = jnp.concatenate([new_value] * heads, axis=0)
    new_score = jnp.sum(query.astype(F32) * new_key, axis=1, keepdims=True) * SCALE
    takes_new = lax.axis_index(CTX) == 0
    peak = jnp.where(takes_new, jnp.maximum(block_max, new_score), block_max)
    factor = jnp.exp(block_max - peak)
    new_factor = jnp.where(takes_new, jnp.exp(new_score - peak), 0.0)
    block_sum = block_sum * factor + new_factor
    block_out = block_out * factor + new_factor * new_value

    lane = lax.broadcasted_iota(jnp.int32, (rows, HEAD_SIZE), 1)
    statistics = jnp.where(lane == 0, peak, block_sum)
    for peer in range(out_ref.shape[0]):
        head = peer // 2
        own = slice(head * requests, (head + 1) * requests)
        out_ref[peer, :requests] = block_out[own]
        out_ref[peer, requests:] = statistics[own]


def merge_and_project(parts_ref, kept_ref, swapped_ref, out_ref):
    peers, requests, width = out_ref.shape
    statistics = parts_ref[:, requests:]
    span_max, span_sum = statistics[:, :, :1], statistics[:, :, 1:2]
    factor = jnp.exp(span_max - jnp.max(span_max, axis=0, keepdims=True))
    merged = jnp.sum(parts_ref[:, :requests] * factor, axis=0)
    attended = merged / jnp.sum(span_sum * factor, axis=0)
    half = HEAD_SIZE // 2
    lower, upper = attended[:, :half].astype(BF16), attended[:, half:].astype(BF16)
    first = lax.axis_index("core") == 0
    own = jnp.where(first, lower, upper)
    other = jnp.where(first, upper, lower)
    result = jnp.dot(own, kept_ref[...], preferred_element_type=F32)
    result += jnp.dot(other, swapped_ref[...], preferred_element_type=F32)
    result = result.astype(BF16)
    columns = result.shape[1] // width
    for peer in range(peers):
        at = peer % columns * width
        out_ref[peer] = result[:, at : at + width]


def from_behind(value, axis, steps):
    count = lax.axis_size(axis)
    return lax.ppermute(value, axis, [(source, (source + steps) % count) for source in range(count)])


def frequencies():
    half_dim = HEAD_SIZE // 2
    frequency = ROPE_BASE ** (-2.0 * np.arange(half_dim) / HEAD_SIZE)
    return np.concatenate([frequency, frequency])[None, :].astype(np.float32)


def per_device(
    hidden,
    gain,
    w_query,
    key_weight,
    value_weight,
    w_out,
    key_cache_slots,
    value_cache_slots,
    lengths,
    plan,
    routing,
):
    requests, width = hidden.shape
    ctx_count = lax.axis_size(CTX)
    packed_width = w_query.shape[2] + 2 * key_weight.shape[2] + HEAD_SIZE
    sources = (
        lengths,
        jnp.transpose(plan, (1, 2, 0)),
        jnp.asarray(frequencies()),
        gain,
        hidden,
        w_query,
        key_weight,
        value_weight,
        w_out,
    )
    half_shape = (w_out.shape[1], w_out.shape[2] // 2)
    hidden, scaled, squares, table, w_query, key_weight, value_weight, w_sent, w_kept = pl.pallas_call(
        fetch,
        out_shape=(
            pltpu.VMEM(hidden.shape, BF16),
            pltpu.VMEM(hidden.shape, BF16),
            pltpu.VMEM((requests, HEAD_SIZE), F32),
            pltpu.VMEM((requests, 3 * HEAD_SIZE), F32),
            pltpu.VMEM(w_query.shape, BF16),
            pltpu.VMEM(key_weight.shape, BF16),
            pltpu.VMEM(value_weight.shape, BF16),
            pltpu.VMEM(half_shape, BF16),
            pltpu.VMEM(half_shape, BF16),
        ),
        in_specs=[whole(pltpu.HBM)] * len(FETCH_INPUTS),
        out_specs=(whole(),) * len(FETCH_OUTPUTS),
        scratch_shapes=[
            (pltpu.SMEM if source.dtype == jnp.int32 else pltpu.VMEM)(source.shape, source.dtype)
            for source in sources[:4]
        ]
        + [pltpu.SemaphoreType.DMA((len(sources) - 1 + 2 * CHIPS,))],
        name="fetch",
        compiler_params=pltpu.CompilerParams(vmem_limit_bytes=8 * 2**20),
    )(*[pltpu.with_memory_space_constraint(source, pltpu.HBM) for source in sources])
    w_swapped = from_behind(w_sent, "core", 1)
    parts = pl.pallas_call(
        project,
        out_shape=pltpu.VMEM((ctx_count, requests, packed_width), F32),
        in_specs=[whole()] * 5,
        out_specs=whole(),
        name="project",
        compiler_params=pltpu.CompilerParams(vmem_limit_bytes=8 * 2**20),
    )(*[in_vmem(value) for value in (scaled, squares, w_query, key_weight, value_weight)])
    parts = lax.all_to_all(parts, CTX, 0, 0, tiled=True)
    spans = pl.pallas_call(
        functools.partial(attend, width * ctx_count),
        out_shape=pltpu.VMEM((ctx_count, 2 * requests, HEAD_SIZE), F32),
        in_specs=[whole()] * 4,
        out_specs=whole(),
        name="attend",
        compiler_params=pltpu.CompilerParams(vmem_limit_bytes=8 * 2**20),
    )(in_vmem(parts), in_vmem(table), key_cache_slots, value_cache_slots)
    spans = lax.all_to_all(spans, CTX, 0, 0, tiled=True)
    pieces = pl.pallas_call(
        merge_and_project,
        out_shape=pltpu.VMEM((lax.axis_size(LAST), requests, width), BF16),
        in_specs=[whole()] * 3,
        out_specs=whole(),
        name="merge_and_project",
        compiler_params=pltpu.CompilerParams(vmem_limit_bytes=8 * 2**20),
    )(in_vmem(spans), in_vmem(w_kept), in_vmem(w_swapped))
    pieces = lax.all_to_all(pieces, LAST, 0, 0, tiled=True)
    section_rows = (hidden.astype(F32) + pieces.astype(F32).sum(axis=0)).astype(BF16)
    section_rows, pieces = lax.optimization_barrier((section_rows, pieces))
    arrived = from_behind(section_rows, "section", 1)
    branch_out = pieces.astype(F32).sum(axis=0)
    selector = (routing[0][:, None] == jnp.arange(requests, dtype=jnp.int32)[None, :]).astype(BF16)
    handed = jnp.dot(selector, arrived, preferred_element_type=F32).astype(BF16)
    return (handed, branch_out)


def solution(mesh):
    sizes = mesh.shape
    devices = mesh.devices.reshape(sizes["section"], sizes["tp"], 2, 2, 2)
    mesh = jax.sharding.Mesh(devices, ("section", "tp") + CTX)
    return jax.shard_map(
        per_device,
        mesh=mesh,
        in_specs=(
            P("section", CTX),
            P("section", CTX),
            P("section", CTX, "tp"),
            P("section", CTX, "tp"),
            P("section", CTX, "tp"),
            P("section", ("tp",) + CTX, None),
            P("section", CTX, "tp"),
            P("section", CTX, "tp"),
            P("section"),
            P("section", CTX, None),
            P("section", None),
        ),
        out_specs=(P("section", CTX), P("section", CTX)),
        check_vma=False,
    )
```

```python
import functools

import jax
import jax.numpy as jnp
import numpy as np
from jax import lax
from jax.experimental import pallas as pl
from jax.experimental.pallas import tpu as pltpu
from jax.sharding import PartitionSpec as P

HEAD_SIZE = 128
EPSILON = 1e-05
NEGATIVE = -1e30
ROPE_BASE = 500000.0
CTX = ("far", "near", "core")
LAST = ("tp", "far", "near")
CHIPS = 4
SCALE = HEAD_SIZE ** (-0.5)
FETCH_INPUTS = (
    "lengths",
    "plan",
    "routing",
    "frequency",
    "gain",
    "hidden",
    "w_query",
    "w_key",
    "w_value",
    "w_out",
)
FETCH_OUTPUTS = (
    "hidden",
    "scaled",
    "squares",
    "table",
    "order",
    "w_query",
    "w_key",
    "w_value",
    "w_sent",
    "w_kept",
)
F32 = jnp.float32
BF16 = jnp.bfloat16


def whole(memory_space=pltpu.VMEM):
    return pl.BlockSpec(memory_space=memory_space)


def in_vmem(value):
    return pltpu.with_memory_space_constraint(value, pltpu.VMEM)


def fetch(*refs):
    count = len(FETCH_INPUTS)
    outputs = dict(zip(FETCH_OUTPUTS, refs[count:]))
    scratch = refs[count + len(FETCH_OUTPUTS) :]
    lengths_ref, plan_ref, routing_ref, frequency_ref, gain_ref, hidden_ref, semaphores = scratch
    held = dict(outputs, **dict(zip(FETCH_INPUTS, scratch[:-1])))
    sources = dict(zip(FETCH_INPUTS, refs))
    w_ref = sources.pop("w_out")
    core, width = lax.axis_index("core"), outputs["w_kept"].shape[1] // CHIPS
    for name, whose in (("w_sent", 1 - core), ("w_kept", core)):
        for chip in range(CHIPS):
            start = pl.multiple_of((2 * chip + whose) * width, HEAD_SIZE)
            at = pl.ds(chip * width, width)
            sources[name, chip] = w_ref.at[0, :, pl.ds(start, width)]
            held[name, chip] = outputs[name].at[:, at]
    copies = {
        name: pltpu.make_async_copy(source, held[name], semaphores.at[at])
        for at, (name, source) in enumerate(sources.items())
    }
    for copy in copies.values():
        copy.start()

    for name in ("lengths", "plan", "routing", "frequency", "hidden", "gain"):
        copies[name].wait()
    hidden = hidden_ref[...].astype(F32)
    requests = hidden.shape[0]
    outputs["hidden"][...] = hidden
    outputs["scaled"][...] = (hidden * gain_ref[...]).astype(BF16).astype(F32)
    squares = jnp.sum(hidden * hidden, axis=1, keepdims=True)
    outputs["squares"][...] = jnp.broadcast_to(squares, (requests, HEAD_SIZE))
    row = lax.broadcasted_iota(jnp.int32, (requests, HEAD_SIZE), 0)
    lane = lax.broadcasted_iota(jnp.int32, (requests, HEAD_SIZE), 1)
    length = jnp.zeros((requests, HEAD_SIZE), jnp.int32)
    live = jnp.zeros((requests, HEAD_SIZE), jnp.int32)
    order = jnp.zeros((requests, HEAD_SIZE), jnp.int32)
    for request in range(requests):
        length = jnp.where(row == request, lengths_ref[request], length)
        live = jnp.where(row == request, plan_ref[0, 1, request] - plan_ref[0, 0, request], live)
        order = jnp.where(row == request, routing_ref[0, request], order)
    outputs["order"][...] = order
    angles = length.astype(F32) * frequency_ref[...]
    sine = jnp.sin(angles)
    table_ref = outputs["table"]
    table_ref[:, :HEAD_SIZE] = jnp.cos(angles)
    table_ref[:, HEAD_SIZE : 2 * HEAD_SIZE] = jnp.where(lane < HEAD_SIZE // 2, -sine, sine)
    table_ref[:, 2 * HEAD_SIZE :] = live.astype(F32)
    for name in ("w_query", "w_key", "w_value"):
        copies.pop(name).wait()
    for name in ("lengths", "plan", "routing", "frequency", "hidden", "gain"):
        copies.pop(name)
    for copy in copies.values():
        copy.wait()


def project(scaled_ref, squares_ref, query_ref, key_ref, value_ref, out_ref):
    scaled = scaled_ref[...].astype(BF16)
    at = 0
    for ref in (query_ref, key_ref, value_ref):
        part = jnp.dot(scaled, ref[0], preferred_element_type=F32)
        width = part.shape[1]
        for peer in range(out_ref.shape[0]):
            out_ref[peer, :, at : at + width] = part
        at += width
    squares = squares_ref[...]
    for peer in range(out_ref.shape[0]):
        out_ref[peer, :, at:] = squares


def attend(model_width, parts_ref, table_ref, keys_ref, values_ref, out_ref):
    total = parts_ref[0]
    for peer in range(1, parts_ref.shape[0]):
        total = total + parts_ref[peer]
    requests, heads = keys_ref.shape[0], 4
    rows = heads * requests
    slots = keys_ref.shape[1]
    squares = total[:, 6 * HEAD_SIZE : 6 * HEAD_SIZE + 1]
    inverse = lax.rsqrt(squares / model_width + EPSILON)
    cosine = table_ref[:, :HEAD_SIZE]
    sine = table_ref[:, HEAD_SIZE : 2 * HEAD_SIZE]

    def rotated(at):
        part = total[:, at * HEAD_SIZE : (at + 1) * HEAD_SIZE] * inverse
        return part * cosine + pltpu.roll(part, HEAD_SIZE // 2, 1) * sine

    query = jnp.concatenate([rotated(head) for head in range(heads)], axis=0).astype(BF16)
    new_key = rotated(heads).astype(BF16).astype(F32)
    new_value = total[:, 5 * HEAD_SIZE : 6 * HEAD_SIZE] * inverse
    new_value = new_value.astype(BF16).astype(F32)
    request_of_row = lax.broadcasted_iota(jnp.int32, (rows, 1), 0) % requests

    scores = jnp.zeros((rows, slots), F32)
    for request in range(requests):
        own = lax.dot_general(
            query, keys_ref[request], (((1,), (1,)), ((), ())), preferred_element_type=F32
        )
        scores = jnp.where(request_of_row == request, own, scores)
    counts = jnp.concatenate([table_ref[:, 2 * HEAD_SIZE : 2 * HEAD_SIZE + 1]] * heads, axis=0)
    slot = lax.broadcasted_iota(jnp.int32, (rows, slots), 1)
    live = slot < counts.astype(jnp.int32)
    scores = jnp.where(live, scores * SCALE, NEGATIVE)
    block_max = jnp.max(scores, axis=1, keepdims=True)
    weights = jnp.where(live, jnp.exp(scores - block_max), 0.0)
    block_sum = jnp.sum(weights, axis=1, keepdims=True)
    weights = weights.astype(BF16)
    block_out = jnp.zeros((rows, HEAD_SIZE), F32)
    for request in range(requests):
        own = jnp.dot(weights, values_ref[request], preferred_element_type=F32)
        block_out = jnp.where(request_of_row == request, own, block_out)

    new_key = jnp.concatenate([new_key] * heads, axis=0)
    new_value = jnp.concatenate([new_value] * heads, axis=0)
    new_score = jnp.sum(query.astype(F32) * new_key, axis=1, keepdims=True) * SCALE
    takes_new = lax.axis_index(CTX) == 0
    peak = jnp.where(takes_new, jnp.maximum(block_max, new_score), block_max)
    factor = jnp.exp(block_max - peak)
    new_factor = jnp.where(takes_new, jnp.exp(new_score - peak), 0.0)
    block_sum = block_sum * factor + new_factor
    block_out = block_out * factor + new_factor * new_value

    lane = lax.broadcasted_iota(jnp.int32, (rows, HEAD_SIZE), 1)
    statistics = jnp.where(lane == 0, peak, block_sum)
    for peer in range(out_ref.shape[0]):
        head = peer // 2
        own = slice(head * requests, (head + 1) * requests)
        out_ref[peer, :requests] = block_out[own]
        out_ref[peer, requests:] = statistics[own]


def merge_and_project(parts_ref, kept_ref, swapped_ref, out_ref):
    peers, requests, width = out_ref.shape
    statistics = parts_ref[:, requests:]
    span_max, span_sum = statistics[:, :, :1], statistics[:, :, 1:2]
    factor = jnp.exp(span_max - jnp.max(span_max, axis=0, keepdims=True))
    merged = jnp.sum(parts_ref[:, :requests] * factor, axis=0)
    attended = merged / jnp.sum(span_sum * factor, axis=0)
    half = HEAD_SIZE // 2
    lower, upper = attended[:, :half].astype(BF16), attended[:, half:].astype(BF16)
    first = lax.axis_index("core") == 0
    own = jnp.where(first, lower, upper)
    other = jnp.where(first, upper, lower)
    result = jnp.dot(own, kept_ref[...], preferred_element_type=F32)
    result += jnp.dot(other, swapped_ref[...], preferred_element_type=F32)
    result = result.astype(BF16)
    columns = result.shape[1] // width
    for peer in range(peers):
        at = peer % columns * width
        out_ref[peer] = result[:, at : at + width]


def reorder(arrived_ref, order_ref, out_ref):
    arrived = arrived_ref[...].astype(F32)
    order = order_ref[:, :1]
    result = jnp.zeros_like(arrived)
    for request in range(arrived.shape[0]):
        result = jnp.where(order == request, arrived[request : request + 1], result)
    out_ref[...] = result.astype(BF16)


def from_behind(value, axis, steps):
    count = lax.axis_size(axis)
    return lax.ppermute(value, axis, [(source, (source + steps) % count) for source in range(count)])


def frequencies():
    half_dim = HEAD_SIZE // 2
    frequency = ROPE_BASE ** (-2.0 * np.arange(half_dim) / HEAD_SIZE)
    return np.concatenate([frequency, frequency])[None, :].astype(np.float32)


def per_device(
    hidden,
    gain,
    w_query,
    key_weight,
    value_weight,
    w_out,
    key_cache_slots,
    value_cache_slots,
    lengths,
    plan,
    routing,
):
    requests, width = hidden.shape
    ctx_count = lax.axis_size(CTX)
    packed_width = w_query.shape[2] + 2 * key_weight.shape[2] + HEAD_SIZE
    sources = (
        lengths,
        jnp.transpose(plan, (1, 2, 0)),
        routing,
        jnp.asarray(frequencies()),
        gain,
        hidden,
        w_query,
        key_weight,
        value_weight,
        w_out,
    )
    half_shape = (w_out.shape[1], w_out.shape[2] // 2)
    hidden, scaled, squares, table, order, w_query, key_weight, value_weight, w_sent, w_kept = pl.pallas_call(
        fetch,
        out_shape=(
            pltpu.VMEM(hidden.shape, F32),
            pltpu.VMEM(hidden.shape, F32),
            pltpu.VMEM((requests, HEAD_SIZE), F32),
            pltpu.VMEM((requests, 3 * HEAD_SIZE), F32),
            pltpu.VMEM((requests, HEAD_SIZE), jnp.int32),
            pltpu.VMEM(w_query.shape, BF16),
            pltpu.VMEM(key_weight.shape, BF16),
            pltpu.VMEM(value_weight.shape, BF16),
            pltpu.VMEM(half_shape, BF16),
            pltpu.VMEM(half_shape, BF16),
        ),
        in_specs=[whole(pltpu.HBM)] * len(FETCH_INPUTS),
        out_specs=(whole(),) * len(FETCH_OUTPUTS),
        scratch_shapes=[
            (pltpu.SMEM if source.dtype == jnp.int32 else pltpu.VMEM)(source.shape, source.dtype)
            for source in sources[:6]
        ]
        + [pltpu.SemaphoreType.DMA((len(sources) - 1 + 2 * CHIPS,))],
        name="fetch",
        compiler_params=pltpu.CompilerParams(vmem_limit_bytes=8 * 2**20),
    )(*[pltpu.with_memory_space_constraint(source, pltpu.HBM) for source in sources])
    w_swapped = from_behind(w_sent, "core", 1)
    parts = pl.pallas_call(
        project,
        out_shape=pltpu.VMEM((ctx_count, requests, packed_width), F32),
        in_specs=[whole()] * 5,
        out_specs=whole(),
        name="project",
        compiler_params=pltpu.CompilerParams(vmem_limit_bytes=8 * 2**20),
    )(*[in_vmem(value) for value in (scaled, squares, w_query, key_weight, value_weight)])
    parts = lax.all_to_all(parts, CTX, 0, 0, tiled=True)
    spans = pl.pallas_call(
        functools.partial(attend, width * ctx_count),
        out_shape=pltpu.VMEM((ctx_count, 2 * requests, HEAD_SIZE), F32),
        in_specs=[whole()] * 4,
        out_specs=whole(),
        name="attend",
        compiler_params=pltpu.CompilerParams(vmem_limit_bytes=8 * 2**20),
    )(in_vmem(parts), in_vmem(table), key_cache_slots, value_cache_slots)
    spans = lax.all_to_all(spans, CTX, 0, 0, tiled=True)
    pieces = pl.pallas_call(
        merge_and_project,
        out_shape=pltpu.VMEM((lax.axis_size(LAST), requests, width), BF16),
        in_specs=[whole()] * 3,
        out_specs=whole(),
        name="merge_and_project",
        compiler_params=pltpu.CompilerParams(vmem_limit_bytes=8 * 2**20),
    )(in_vmem(spans), in_vmem(w_kept), in_vmem(w_swapped))
    pieces = lax.all_to_all(pieces, LAST, 0, 0, tiled=True)
    section_rows = (hidden + pieces.astype(F32).sum(axis=0)).astype(BF16)
    section_rows, pieces = lax.optimization_barrier((section_rows, pieces))
    arrived = from_behind(section_rows, "section", 1)
    branch_out = pieces.astype(F32).sum(axis=0)
    handed = pl.pallas_call(
        reorder,
        out_shape=jax.ShapeDtypeStruct(arrived.shape, BF16),
        in_specs=[whole()] * 2,
        out_specs=whole(),
        name="reorder",
        compiler_params=pltpu.CompilerParams(vmem_limit_bytes=8 * 2**20),
    )(in_vmem(arrived), in_vmem(order))
    return (handed, branch_out)


def solution(mesh):
    sizes = mesh.shape
    devices = mesh.devices.reshape(sizes["section"], sizes["tp"], 2, 2, 2)
    mesh = jax.sharding.Mesh(devices, ("section", "tp") + CTX)
    return jax.shard_map(
        per_device,
        mesh=mesh,
        in_specs=(
            P("section", CTX),
            P("section", CTX),
            P("section", CTX, "tp"),
            P("section", CTX, "tp"),
            P("section", CTX, "tp"),
            P("section", ("tp",) + CTX, None),
            P("section", CTX, "tp"),
            P("section", CTX, "tp"),
            P("section"),
            P("section", CTX, None),
            P("section", None),
        ),
        out_specs=(P("section", CTX), P("section", CTX)),
        check_vma=False,
    )
```

```python
import functools

import jax
import jax.numpy as jnp
import numpy as np
from jax import lax
from jax.experimental import pallas as pl
from jax.experimental.pallas import tpu as pltpu
from jax.sharding import PartitionSpec as P

HEAD_SIZE = 128
EPSILON = 1e-05
NEGATIVE = -1e30
ROPE_BASE = 500000.0
CTX = ("far", "near", "core")
LAST = ("far", "near", "tp")
CHIPS = 4
SCALE = HEAD_SIZE ** (-0.5)
FETCH_INPUTS = (
    "lengths",
    "plan",
    "frequency",
    "gain",
    "hidden",
    "w_query",
    "w_key",
    "w_value",
    "w_out",
)
FETCH_OUTPUTS = (
    "hidden",
    "scaled",
    "squares",
    "table",
    "w_query",
    "w_key",
    "w_value",
    "w_sent",
    "w_kept",
)
F32 = jnp.float32
BF16 = jnp.bfloat16


def whole(memory_space=pltpu.VMEM):
    return pl.BlockSpec(memory_space=memory_space)


def in_vmem(value):
    return pltpu.with_memory_space_constraint(value, pltpu.VMEM)


def fetch(*refs):
    count = len(FETCH_INPUTS)
    outputs = dict(zip(FETCH_OUTPUTS, refs[count:]))
    lengths_ref, plan_ref, frequency_ref, gain_ref, semaphores = refs[count + len(FETCH_OUTPUTS) :]
    held = dict(outputs, lengths=lengths_ref, plan=plan_ref, frequency=frequency_ref, gain=gain_ref)
    sources = dict(zip(FETCH_INPUTS, refs))
    w_ref = sources.pop("w_out")
    core, width = lax.axis_index("core"), outputs["w_kept"].shape[1] // CHIPS
    for name, whose in (("w_sent", 1 - core), ("w_kept", core)):
        for chip in range(CHIPS):
            start = pl.multiple_of((2 * chip + whose) * width, HEAD_SIZE)
            at = pl.ds(chip * width, width)
            sources[name, chip] = w_ref.at[0, :, pl.ds(start, width)]
            held[name, chip] = outputs[name].at[:, at]
    copies = {
        name: pltpu.make_async_copy(source, held[name], semaphores.at[at])
        for at, (name, source) in enumerate(sources.items())
    }
    for copy in copies.values():
        copy.start()

    for name in ("lengths", "plan", "frequency", "hidden", "gain"):
        copies[name].wait()
    hidden = held["hidden"][...].astype(F32)
    requests = hidden.shape[0]
    outputs["scaled"][...] = (hidden * gain_ref[...]).astype(BF16)
    squares = jnp.sum(hidden * hidden, axis=1, keepdims=True)
    outputs["squares"][...] = jnp.broadcast_to(squares, (requests, HEAD_SIZE))
    row = lax.broadcasted_iota(jnp.int32, (requests, HEAD_SIZE), 0)
    lane = lax.broadcasted_iota(jnp.int32, (requests, HEAD_SIZE), 1)
    length = jnp.zeros((requests, HEAD_SIZE), jnp.int32)
    live = jnp.zeros((requests, HEAD_SIZE), jnp.int32)
    for request in range(requests):
        length = jnp.where(row == request, lengths_ref[request], length)
        live = jnp.where(row == request, plan_ref[0, 1, request] - plan_ref[0, 0, request], live)
    angles = length.astype(F32) * frequency_ref[...]
    sine = jnp.sin(angles)
    table_ref = outputs["table"]
    table_ref[:, :HEAD_SIZE] = jnp.cos(angles)
    table_ref[:, HEAD_SIZE : 2 * HEAD_SIZE] = jnp.where(lane < HEAD_SIZE // 2, -sine, sine)
    table_ref[:, 2 * HEAD_SIZE :] = live.astype(F32)
    for name in ("w_query", "w_key", "w_value"):
        copies.pop(name).wait()
    for name in ("lengths", "plan", "frequency", "hidden", "gain"):
        copies.pop(name)
    for copy in copies.values():
        copy.wait()


def project(scaled_ref, squares_ref, query_ref, key_ref, value_ref, out_ref):
    scaled = scaled_ref[...]
    at = 0
    for ref in (query_ref, key_ref, value_ref):
        part = jnp.dot(scaled, ref[0], preferred_element_type=F32)
        width = part.shape[1]
        for peer in range(out_ref.shape[0]):
            out_ref[peer, :, at : at + width] = part
        at += width
    squares = squares_ref[...]
    for peer in range(out_ref.shape[0]):
        out_ref[peer, :, at:] = squares


def attend(model_width, parts_ref, table_ref, keys_ref, values_ref, out_ref):
    total = parts_ref[0]
    for peer in range(1, parts_ref.shape[0]):
        total = total + parts_ref[peer]
    requests, heads = keys_ref.shape[0], 4
    rows = heads * requests
    slots = keys_ref.shape[1]
    squares = total[:, 6 * HEAD_SIZE : 6 * HEAD_SIZE + 1]
    inverse = lax.rsqrt(squares / model_width + EPSILON)
    cosine = table_ref[:, :HEAD_SIZE]
    sine = table_ref[:, HEAD_SIZE : 2 * HEAD_SIZE]

    def rotated(at):
        part = total[:, at * HEAD_SIZE : (at + 1) * HEAD_SIZE] * inverse
        return part * cosine + pltpu.roll(part, HEAD_SIZE // 2, 1) * sine

    query = jnp.concatenate([rotated(head) for head in range(heads)], axis=0).astype(BF16)
    new_key = rotated(heads).astype(BF16).astype(F32)
    new_value = total[:, 5 * HEAD_SIZE : 6 * HEAD_SIZE] * inverse
    new_value = new_value.astype(BF16).astype(F32)
    request_of_row = lax.broadcasted_iota(jnp.int32, (rows, 1), 0) % requests

    scores = jnp.zeros((rows, slots), F32)
    for request in range(requests):
        own = lax.dot_general(
            query, keys_ref[request], (((1,), (1,)), ((), ())), preferred_element_type=F32
        )
        scores = jnp.where(request_of_row == request, own, scores)
    counts = jnp.concatenate([table_ref[:, 2 * HEAD_SIZE : 2 * HEAD_SIZE + 1]] * heads, axis=0)
    slot = lax.broadcasted_iota(jnp.int32, (rows, slots), 1)
    live = slot < counts.astype(jnp.int32)
    scores = jnp.where(live, scores * SCALE, NEGATIVE)
    block_max = jnp.max(scores, axis=1, keepdims=True)
    weights = jnp.where(live, jnp.exp(scores - block_max), 0.0)
    block_sum = jnp.sum(weights, axis=1, keepdims=True)
    weights = weights.astype(BF16)
    block_out = jnp.zeros((rows, HEAD_SIZE), F32)
    for request in range(requests):
        own = jnp.dot(weights, values_ref[request], preferred_element_type=F32)
        block_out = jnp.where(request_of_row == request, own, block_out)

    new_key = jnp.concatenate([new_key] * heads, axis=0)
    new_value = jnp.concatenate([new_value] * heads, axis=0)
    new_score = jnp.sum(query.astype(F32) * new_key, axis=1, keepdims=True) * SCALE
    takes_new = lax.axis_index(CTX) == 0
    peak = jnp.where(takes_new, jnp.maximum(block_max, new_score), block_max)
    factor = jnp.exp(block_max - peak)
    new_factor = jnp.where(takes_new, jnp.exp(new_score - peak), 0.0)
    block_sum = block_sum * factor + new_factor
    block_out = block_out * factor + new_factor * new_value

    lane = lax.broadcasted_iota(jnp.int32, (rows, HEAD_SIZE), 1)
    statistics = jnp.where(lane == 0, peak, block_sum)
    for peer in range(out_ref.shape[0]):
        head = peer // 2
        own = slice(head * requests, (head + 1) * requests)
        out_ref[peer, :requests] = block_out[own]
        out_ref[peer, requests:] = statistics[own]


def merge_and_project(parts_ref, kept_ref, swapped_ref, out_ref):
    peers, requests, width = out_ref.shape
    statistics = parts_ref[:, requests:]
    span_max, span_sum = statistics[:, :, :1], statistics[:, :, 1:2]
    factor = jnp.exp(span_max - jnp.max(span_max, axis=0, keepdims=True))
    merged = jnp.sum(parts_ref[:, :requests] * factor, axis=0)
    attended = merged / jnp.sum(span_sum * factor, axis=0)
    half = HEAD_SIZE // 2
    lower, upper = attended[:, :half].astype(BF16), attended[:, half:].astype(BF16)
    first = lax.axis_index("core") == 0
    own = jnp.where(first, lower, upper)
    other = jnp.where(first, upper, lower)
    result = jnp.dot(own, kept_ref[...], preferred_element_type=F32)
    result += jnp.dot(other, swapped_ref[...], preferred_element_type=F32)
    result = result.astype(BF16)
    columns = result.shape[1] // width
    for peer in range(peers):
        at = peer // (peers // columns) * width
        out_ref[peer] = result[:, at : at + width]


def from_behind(value, axis, steps):
    count = lax.axis_size(axis)
    return lax.ppermute(value, axis, [(source, (source + steps) % count) for source in range(count)])


def frequencies():
    half_dim = HEAD_SIZE // 2
    frequency = ROPE_BASE ** (-2.0 * np.arange(half_dim) / HEAD_SIZE)
    return np.concatenate([frequency, frequency])[None, :].astype(np.float32)


def per_device(
    hidden,
    gain,
    w_query,
    key_weight,
    value_weight,
    w_out,
    key_cache_slots,
    value_cache_slots,
    lengths,
    plan,
    routing,
):
    requests, width = hidden.shape
    ctx_count = lax.axis_size(CTX)
    packed_width = w_query.shape[2] + 2 * key_weight.shape[2] + HEAD_SIZE
    sources = (
        lengths,
        jnp.transpose(plan, (1, 2, 0)),
        jnp.asarray(frequencies()),
        gain,
        hidden,
        w_query,
        key_weight,
        value_weight,
        w_out,
    )
    half_shape = (w_out.shape[1], w_out.shape[2] // 2)
    hidden, scaled, squares, table, w_query, key_weight, value_weight, w_sent, w_kept = pl.pallas_call(
        fetch,
        out_shape=(
            pltpu.VMEM(hidden.shape, BF16),
            pltpu.VMEM(hidden.shape, BF16),
            pltpu.VMEM((requests, HEAD_SIZE), F32),
            pltpu.VMEM((requests, 3 * HEAD_SIZE), F32),
            pltpu.VMEM(w_query.shape, BF16),
            pltpu.VMEM(key_weight.shape, BF16),
            pltpu.VMEM(value_weight.shape, BF16),
            pltpu.VMEM(half_shape, BF16),
            pltpu.VMEM(half_shape, BF16),
        ),
        in_specs=[whole(pltpu.HBM)] * len(FETCH_INPUTS),
        out_specs=(whole(),) * len(FETCH_OUTPUTS),
        scratch_shapes=[
            (pltpu.SMEM if source.dtype == jnp.int32 else pltpu.VMEM)(source.shape, source.dtype)
            for source in sources[:4]
        ]
        + [pltpu.SemaphoreType.DMA((len(sources) - 1 + 2 * CHIPS,))],
        name="fetch",
        compiler_params=pltpu.CompilerParams(vmem_limit_bytes=8 * 2**20),
    )(*[pltpu.with_memory_space_constraint(source, pltpu.HBM) for source in sources])
    w_swapped = from_behind(w_sent, "core", 1)
    parts = pl.pallas_call(
        project,
        out_shape=pltpu.VMEM((ctx_count, requests, packed_width), F32),
        in_specs=[whole()] * 5,
        out_specs=whole(),
        name="project",
        compiler_params=pltpu.CompilerParams(vmem_limit_bytes=8 * 2**20),
    )(*[in_vmem(value) for value in (scaled, squares, w_query, key_weight, value_weight)])
    parts = lax.all_to_all(parts, CTX, 0, 0, tiled=True)
    spans = pl.pallas_call(
        functools.partial(attend, width * ctx_count),
        out_shape=pltpu.VMEM((ctx_count, 2 * requests, HEAD_SIZE), F32),
        in_specs=[whole()] * 4,
        out_specs=whole(),
        name="attend",
        compiler_params=pltpu.CompilerParams(vmem_limit_bytes=8 * 2**20),
    )(in_vmem(parts), in_vmem(table), key_cache_slots, value_cache_slots)
    spans = lax.all_to_all(spans, CTX, 0, 0, tiled=True)
    pieces = pl.pallas_call(
        merge_and_project,
        out_shape=pltpu.VMEM((lax.axis_size(LAST), requests, width), BF16),
        in_specs=[whole()] * 3,
        out_specs=whole(),
        name="merge_and_project",
        compiler_params=pltpu.CompilerParams(vmem_limit_bytes=8 * 2**20),
    )(in_vmem(spans), in_vmem(w_kept), in_vmem(w_swapped))
    pieces = lax.all_to_all(pieces, LAST, 0, 0, tiled=True)
    section_rows = (hidden.astype(F32) + pieces.astype(F32).sum(axis=0)).astype(BF16)
    section_rows, pieces = lax.optimization_barrier((section_rows, pieces))
    arrived = from_behind(section_rows, "section", 1)
    branch_out = pieces.astype(F32).sum(axis=0)
    selector = (routing[0][:, None] == jnp.arange(requests, dtype=jnp.int32)[None, :]).astype(BF16)
    handed = jnp.dot(selector, arrived, preferred_element_type=F32).astype(BF16)
    return (handed, branch_out)


def solution(mesh):
    sizes = mesh.shape
    devices = mesh.devices.reshape(sizes["section"], sizes["tp"], 2, 2, 2)
    mesh = jax.sharding.Mesh(devices, ("section", "tp") + CTX)
    return jax.shard_map(
        per_device,
        mesh=mesh,
        in_specs=(
            P("section", CTX),
            P("section", CTX),
            P("section", CTX, "tp"),
            P("section", CTX, "tp"),
            P("section", CTX, "tp"),
            P("section", ("tp",) + CTX, None),
            P("section", CTX, "tp"),
            P("section", CTX, "tp"),
            P("section"),
            P("section", CTX, None),
            P("section", None),
        ),
        out_specs=(P("section", CTX), P("section", CTX)),
        check_vma=False,
    )
```

```python
import functools

import jax
import jax.numpy as jnp
import numpy as np
from jax import lax
from jax.experimental import pallas as pl
from jax.experimental.pallas import tpu as pltpu
from jax.sharding import PartitionSpec as P

HEAD_SIZE = 128
EPSILON = 1e-05
NEGATIVE = -1e30
ROPE_BASE = 500000.0
CTX = ("far", "near", "core")
LAST = ("far", "near", "tp")
CHIPS = 4
SCALE = HEAD_SIZE ** (-0.5)
FETCH_INPUTS = (
    "lengths",
    "plan",
    "routing",
    "frequency",
    "gain",
    "hidden",
    "w_query",
    "w_key",
    "w_value",
    "w_out",
)
FETCH_OUTPUTS = (
    "hidden",
    "scaled",
    "squares",
    "table",
    "order",
    "w_query",
    "w_key",
    "w_value",
    "w_sent",
    "w_kept",
)
F32 = jnp.float32
BF16 = jnp.bfloat16


def whole(memory_space=pltpu.VMEM):
    return pl.BlockSpec(memory_space=memory_space)


def in_vmem(value):
    return pltpu.with_memory_space_constraint(value, pltpu.VMEM)


def fetch(*refs):
    count = len(FETCH_INPUTS)
    outputs = dict(zip(FETCH_OUTPUTS, refs[count:]))
    scratch = refs[count + len(FETCH_OUTPUTS) :]
    lengths_ref, plan_ref, routing_ref, frequency_ref, gain_ref, hidden_ref, semaphores = scratch
    held = dict(outputs, **dict(zip(FETCH_INPUTS, scratch[:-1])))
    sources = dict(zip(FETCH_INPUTS, refs))
    w_ref = sources.pop("w_out")
    core, width = lax.axis_index("core"), outputs["w_kept"].shape[1] // CHIPS
    for name, whose in (("w_sent", 1 - core), ("w_kept", core)):
        for chip in range(CHIPS):
            start = pl.multiple_of((2 * chip + whose) * width, HEAD_SIZE)
            at = pl.ds(chip * width, width)
            sources[name, chip] = w_ref.at[0, :, pl.ds(start, width)]
            held[name, chip] = outputs[name].at[:, at]
    copies = {
        name: pltpu.make_async_copy(source, held[name], semaphores.at[at])
        for at, (name, source) in enumerate(sources.items())
    }
    for copy in copies.values():
        copy.start()

    for name in ("lengths", "plan", "routing", "frequency", "hidden", "gain"):
        copies[name].wait()
    hidden = hidden_ref[...].astype(F32)
    requests = hidden.shape[0]
    outputs["hidden"][...] = hidden
    outputs["scaled"][...] = (hidden * gain_ref[...]).astype(BF16).astype(F32)
    squares = jnp.sum(hidden * hidden, axis=1, keepdims=True)
    outputs["squares"][...] = jnp.broadcast_to(squares, (requests, HEAD_SIZE))
    row = lax.broadcasted_iota(jnp.int32, (requests, HEAD_SIZE), 0)
    lane = lax.broadcasted_iota(jnp.int32, (requests, HEAD_SIZE), 1)
    length = jnp.zeros((requests, HEAD_SIZE), jnp.int32)
    live = jnp.zeros((requests, HEAD_SIZE), jnp.int32)
    order = jnp.zeros((requests, HEAD_SIZE), jnp.int32)
    for request in range(requests):
        length = jnp.where(row == request, lengths_ref[request], length)
        live = jnp.where(row == request, plan_ref[0, 1, request] - plan_ref[0, 0, request], live)
        order = jnp.where(row == request, routing_ref[0, request], order)
    outputs["order"][...] = order
    angles = length.astype(F32) * frequency_ref[...]
    sine = jnp.sin(angles)
    table_ref = outputs["table"]
    table_ref[:, :HEAD_SIZE] = jnp.cos(angles)
    table_ref[:, HEAD_SIZE : 2 * HEAD_SIZE] = jnp.where(lane < HEAD_SIZE // 2, -sine, sine)
    table_ref[:, 2 * HEAD_SIZE :] = live.astype(F32)
    for name in ("w_query", "w_key", "w_value"):
        copies.pop(name).wait()
    for name in ("lengths", "plan", "routing", "frequency", "hidden", "gain"):
        copies.pop(name)
    for copy in copies.values():
        copy.wait()


def project(scaled_ref, squares_ref, query_ref, key_ref, value_ref, out_ref):
    scaled = scaled_ref[...].astype(BF16)
    at = 0
    for ref in (query_ref, key_ref, value_ref):
        part = jnp.dot(scaled, ref[0], preferred_element_type=F32)
        width = part.shape[1]
        for peer in range(out_ref.shape[0]):
            out_ref[peer, :, at : at + width] = part
        at += width
    squares = squares_ref[...]
    for peer in range(out_ref.shape[0]):
        out_ref[peer, :, at:] = squares


def attend(model_width, parts_ref, table_ref, keys_ref, values_ref, out_ref):
    total = parts_ref[0]
    for peer in range(1, parts_ref.shape[0]):
        total = total + parts_ref[peer]
    requests, heads = keys_ref.shape[0], 4
    rows = heads * requests
    slots = keys_ref.shape[1]
    squares = total[:, 6 * HEAD_SIZE : 6 * HEAD_SIZE + 1]
    inverse = lax.rsqrt(squares / model_width + EPSILON)
    cosine = table_ref[:, :HEAD_SIZE]
    sine = table_ref[:, HEAD_SIZE : 2 * HEAD_SIZE]

    def rotated(at):
        part = total[:, at * HEAD_SIZE : (at + 1) * HEAD_SIZE] * inverse
        return part * cosine + pltpu.roll(part, HEAD_SIZE // 2, 1) * sine

    query = jnp.concatenate([rotated(head) for head in range(heads)], axis=0).astype(BF16)
    new_key = rotated(heads).astype(BF16).astype(F32)
    new_value = total[:, 5 * HEAD_SIZE : 6 * HEAD_SIZE] * inverse
    new_value = new_value.astype(BF16).astype(F32)
    request_of_row = lax.broadcasted_iota(jnp.int32, (rows, 1), 0) % requests

    scores = jnp.zeros((rows, slots), F32)
    for request in range(requests):
        own = lax.dot_general(
            query, keys_ref[request], (((1,), (1,)), ((), ())), preferred_element_type=F32
        )
        scores = jnp.where(request_of_row == request, own, scores)
    counts = jnp.concatenate([table_ref[:, 2 * HEAD_SIZE : 2 * HEAD_SIZE + 1]] * heads, axis=0)
    slot = lax.broadcasted_iota(jnp.int32, (rows, slots), 1)
    live = slot < counts.astype(jnp.int32)
    scores = jnp.where(live, scores * SCALE, NEGATIVE)
    block_max = jnp.max(scores, axis=1, keepdims=True)
    weights = jnp.where(live, jnp.exp(scores - block_max), 0.0)
    block_sum = jnp.sum(weights, axis=1, keepdims=True)
    weights = weights.astype(BF16)
    block_out = jnp.zeros((rows, HEAD_SIZE), F32)
    for request in range(requests):
        own = jnp.dot(weights, values_ref[request], preferred_element_type=F32)
        block_out = jnp.where(request_of_row == request, own, block_out)

    new_key = jnp.concatenate([new_key] * heads, axis=0)
    new_value = jnp.concatenate([new_value] * heads, axis=0)
    new_score = jnp.sum(query.astype(F32) * new_key, axis=1, keepdims=True) * SCALE
    takes_new = lax.axis_index(CTX) == 0
    peak = jnp.where(takes_new, jnp.maximum(block_max, new_score), block_max)
    factor = jnp.exp(block_max - peak)
    new_factor = jnp.where(takes_new, jnp.exp(new_score - peak), 0.0)
    block_sum = block_sum * factor + new_factor
    block_out = block_out * factor + new_factor * new_value

    lane = lax.broadcasted_iota(jnp.int32, (rows, HEAD_SIZE), 1)
    statistics = jnp.where(lane == 0, peak, block_sum)
    for peer in range(out_ref.shape[0]):
        head = peer // 2
        own = slice(head * requests, (head + 1) * requests)
        out_ref[peer, :requests] = block_out[own]
        out_ref[peer, requests:] = statistics[own]


def merge_and_project(parts_ref, kept_ref, swapped_ref, out_ref):
    peers, requests, width = out_ref.shape
    statistics = parts_ref[:, requests:]
    span_max, span_sum = statistics[:, :, :1], statistics[:, :, 1:2]
    factor = jnp.exp(span_max - jnp.max(span_max, axis=0, keepdims=True))
    merged = jnp.sum(parts_ref[:, :requests] * factor, axis=0)
    attended = merged / jnp.sum(span_sum * factor, axis=0)
    half = HEAD_SIZE // 2
    lower, upper = attended[:, :half].astype(BF16), attended[:, half:].astype(BF16)
    first = lax.axis_index("core") == 0
    own = jnp.where(first, lower, upper)
    other = jnp.where(first, upper, lower)
    result = jnp.dot(own, kept_ref[...], preferred_element_type=F32)
    result += jnp.dot(other, swapped_ref[...], preferred_element_type=F32)
    result = result.astype(BF16)
    columns = result.shape[1] // width
    for peer in range(peers):
        at = peer // (peers // columns) * width
        out_ref[peer] = result[:, at : at + width]


def reorder(arrived_ref, order_ref, out_ref):
    arrived = arrived_ref[...].astype(F32)
    order = order_ref[:, :1]
    result = jnp.zeros_like(arrived)
    for request in range(arrived.shape[0]):
        result = jnp.where(order == request, arrived[request : request + 1], result)
    out_ref[...] = result.astype(BF16)


def from_behind(value, axis, steps):
    count = lax.axis_size(axis)
    return lax.ppermute(value, axis, [(source, (source + steps) % count) for source in range(count)])


def frequencies():
    half_dim = HEAD_SIZE // 2
    frequency = ROPE_BASE ** (-2.0 * np.arange(half_dim) / HEAD_SIZE)
    return np.concatenate([frequency, frequency])[None, :].astype(np.float32)


def per_device(
    hidden,
    gain,
    w_query,
    key_weight,
    value_weight,
    w_out,
    key_cache_slots,
    value_cache_slots,
    lengths,
    plan,
    routing,
):
    requests, width = hidden.shape
    ctx_count = lax.axis_size(CTX)
    packed_width = w_query.shape[2] + 2 * key_weight.shape[2] + HEAD_SIZE
    sources = (
        lengths,
        jnp.transpose(plan, (1, 2, 0)),
        routing,
        jnp.asarray(frequencies()),
        gain,
        hidden,
        w_query,
        key_weight,
        value_weight,
        w_out,
    )
    half_shape = (w_out.shape[1], w_out.shape[2] // 2)
    hidden, scaled, squares, table, order, w_query, key_weight, value_weight, w_sent, w_kept = pl.pallas_call(
        fetch,
        out_shape=(
            pltpu.VMEM(hidden.shape, F32),
            pltpu.VMEM(hidden.shape, F32),
            pltpu.VMEM((requests, HEAD_SIZE), F32),
            pltpu.VMEM((requests, 3 * HEAD_SIZE), F32),
            pltpu.VMEM((requests, HEAD_SIZE), jnp.int32),
            pltpu.VMEM(w_query.shape, BF16),
            pltpu.VMEM(key_weight.shape, BF16),
            pltpu.VMEM(value_weight.shape, BF16),
            pltpu.VMEM(half_shape, BF16),
            pltpu.VMEM(half_shape, BF16),
        ),
        in_specs=[whole(pltpu.HBM)] * len(FETCH_INPUTS),
        out_specs=(whole(),) * len(FETCH_OUTPUTS),
        scratch_shapes=[
            (pltpu.SMEM if source.dtype == jnp.int32 else pltpu.VMEM)(source.shape, source.dtype)
            for source in sources[:6]
        ]
        + [pltpu.SemaphoreType.DMA((len(sources) - 1 + 2 * CHIPS,))],
        name="fetch",
        compiler_params=pltpu.CompilerParams(vmem_limit_bytes=8 * 2**20),
    )(*[pltpu.with_memory_space_constraint(source, pltpu.HBM) for source in sources])
    w_swapped = from_behind(w_sent, "core", 1)
    parts = pl.pallas_call(
        project,
        out_shape=pltpu.VMEM((ctx_count, requests, packed_width), F32),
        in_specs=[whole()] * 5,
        out_specs=whole(),
        name="project",
        compiler_params=pltpu.CompilerParams(vmem_limit_bytes=8 * 2**20),
    )(*[in_vmem(value) for value in (scaled, squares, w_query, key_weight, value_weight)])
    parts = lax.all_to_all(parts, CTX, 0, 0, tiled=True)
    spans = pl.pallas_call(
        functools.partial(attend, width * ctx_count),
        out_shape=pltpu.VMEM((ctx_count, 2 * requests, HEAD_SIZE), F32),
        in_specs=[whole()] * 4,
        out_specs=whole(),
        name="attend",
        compiler_params=pltpu.CompilerParams(vmem_limit_bytes=8 * 2**20),
    )(in_vmem(parts), in_vmem(table), key_cache_slots, value_cache_slots)
    spans = lax.all_to_all(spans, CTX, 0, 0, tiled=True)
    pieces = pl.pallas_call(
        merge_and_project,
        out_shape=pltpu.VMEM((lax.axis_size(LAST), requests, width), BF16),
        in_specs=[whole()] * 3,
        out_specs=whole(),
        name="merge_and_project",
        compiler_params=pltpu.CompilerParams(vmem_limit_bytes=8 * 2**20),
    )(in_vmem(spans), in_vmem(w_kept), in_vmem(w_swapped))
    pieces = lax.all_to_all(pieces, LAST, 0, 0, tiled=True)
    section_rows = (hidden + pieces.astype(F32).sum(axis=0)).astype(BF16)
    section_rows, pieces = lax.optimization_barrier((section_rows, pieces))
    arrived = from_behind(section_rows, "section", 1)
    branch_out = pieces.astype(F32).sum(axis=0)
    handed = pl.pallas_call(
        reorder,
        out_shape=jax.ShapeDtypeStruct(arrived.shape, BF16),
        in_specs=[whole()] * 2,
        out_specs=whole(),
        name="reorder",
        compiler_params=pltpu.CompilerParams(vmem_limit_bytes=8 * 2**20),
    )(in_vmem(arrived), in_vmem(order))
    return (handed, branch_out)


def solution(mesh):
    sizes = mesh.shape
    devices = mesh.devices.reshape(sizes["section"], sizes["tp"], 2, 2, 2)
    mesh = jax.sharding.Mesh(devices, ("section", "tp") + CTX)
    return jax.shard_map(
        per_device,
        mesh=mesh,
        in_specs=(
            P("section", CTX),
            P("section", CTX),
            P("section", CTX, "tp"),
            P("section", CTX, "tp"),
            P("section", CTX, "tp"),
            P("section", ("tp",) + CTX, None),
            P("section", CTX, "tp"),
            P("section", CTX, "tp"),
            P("section"),
            P("section", CTX, None),
            P("section", None),
        ),
        out_specs=(P("section", CTX), P("section", CTX)),
        check_vma=False,
    )
```
